32 devices in a mesh: clip: 8 (over y, x, core), tm: 4 (over z).
Axes of the slice: x: 2, y: 2, z: 4, core: 2. Of those that a mesh axis runs over, the one named last changes fastest.
Arguments:
- patches: bfloat16 [8, 768, 512], P('clip', 'tm'), may hold values from -6 to 6
- patch_index: int32 [8, 768], P('clip', 'tm'), may hold values from 0 to 3599
- counts: int32 [8, 4], P('clip', 'tm'), may hold values from 1 to 192, 576 in all within a row
- w_embed: bfloat16 [512, 1024], replicated, may hold values from -0.25 to 0.25
- embed_bias: bfloat16 [1024], replicated, may hold values from -3 to 3
- ln_gain: bfloat16 [1024], replicated, may hold values from 0.099609375 to 1.8984375
- w_qkv: bfloat16 [1024, 3072], P(None, 'tm'), may hold values from -1 to 1
- w_o: bfloat16 [1024, 1024], P('tm'), may hold values from -0.1875 to 0.1875
- cotangent: bfloat16 [8, 768, 1024], P('clip', 'tm'), may hold values from -6 to 6
Outputs:
- encoded: bfloat16 [8, 768, 1024], P('clip', 'tm')
- grad_w_o: float32 [1024, 1024], P('tm')
The draws below stay inside these ranges and needn't reach their ends.
Inputs may be any that keep to these rules, and one draw needn't show every extreme that they name: Entry [c, b] is the number of visible tokens of clip c in time bin b, held in the first slots of that bin's 192; each clip's counts sum to 576, and in each clip one bin is full. `patch_index`: patch number is row times 80 plus column; entries of slots that are not valid are ignored.
All inputs are finite; a program needn't handle non-finite values. No bound on the sum of `counts` on one device may be relied on, other than what follows from the above.
Results may differ from the reference program's by a relative error of at most 0.02.
Values may be sent and summed in bfloat16 or wider, within the bound.
No kernel may reach another device: no remote copies, remote signals or barrier semaphores. Data moves between devices by JAX's collectives and lax.ppermute only.
A program may use at most 64 MiB of HBM per device.

```python
import math
import jax
import jax.numpy as jnp
import numpy as np
from jax import lax

D = 1024
HEADS = 16
HEAD_DIM = 64
PATCH_DIM = 512
PATCH_COLS = 80
VIS_DEV = 192
BINS = 4
SLOTS = 768
CLIPS = 8
PATCHES = 3600


def draw_w_qkv(key, part):
    key = jax.random.fold_in(key, 7)
    spread = D ** (-0.5)
    base = jax.random.normal(key, (D, HEADS, 3, HEAD_DIM), jnp.float32) * spread
    return base.reshape(D, 3 * D).astype(jnp.bfloat16)


def with_ends(result, key, low, high):
    dims = result.shape
    spot = [jax.random.randint(jax.random.fold_in(key, axis), (), 0, dims[axis]) for axis in range(len(dims))]
    result = result.at[tuple(spot)].set(low)
    longest = dims.index(max(dims))
    spot[longest] = (spot[longest] + 1) % dims[longest]
    return result.at[tuple(spot)].set(high)


def levels(key, dims, shards, smallest, largest):
    level, own = 1.0, jax.random.fold_in(key, 6)
    for dim, blocks in shards:
        draws = jnp.exp(jax.random.uniform(jax.random.fold_in(own, dim), (blocks,), jnp.float32, smallest / len(shards), largest / len(shards)))
        level = level * jnp.repeat(draws, dims[dim] // blocks).reshape([-1 if axis == dim else 1 for axis in range(len(dims))])
    return level


def split_up(amount, total, reach, slope):
    weights = [(1 << 20) // math.isqrt(grade ** slope) + 1 for grade in range(2, amount + 1)]
    rest, given = total - reach - (amount - 1), [1] * (amount - 1)
    while rest > 0:
        free = [i for i in range(amount - 1) if given[i] < reach]
        whole, budget = sum([weights[i] for i in free]), rest
        for i in free:
            extra = min(reach - given[i], max(1, budget * weights[i] // whole), rest)
            given[i] = given[i] + extra
            rest = rest - extra
    return np.array([reach] + given)


def uneven_parts(stream_key, amount, total, reach, skew):
    if amount == 2:
        one = jax.random.randint(stream_key, (), max(1, total - reach), min(reach, total - 1) + 1)
        return jnp.stack([one, total - one])
    tallies = jnp.asarray(split_up(amount, total, reach, skew), jnp.int32)
    couples = (amount - 1) // 2
    giver, receiver = tallies[1:1 + 2 * couples:2], tallies[2:2 + 2 * couples:2]
    margin = jnp.minimum(giver - 1, reach - receiver)
    moved = jax.random.randint(jax.random.fold_in(stream_key, 1), (couples,), 0, 1 << 20) % (margin + 1)
    tallies = tallies.at[1:1 + 2 * couples:2].set(giver - moved).at[2:2 + 2 * couples:2].set(receiver + moved)
    return tallies[jax.random.permutation(jax.random.fold_in(stream_key, 2), amount)]


def scatter_about(own_key, dims, scale, limit, cuts=(), held_as=jnp.bfloat16):
    result = jax.random.normal(own_key, dims, jnp.float32) * scale
    if len(cuts) > 0:
        result = levels(own_key, dims, cuts, -0.22, 0.18) * result
    return jnp.clip(result, min=-limit, max=limit).astype(held_as)


def setup_inputs(seed: int = 0) -> dict:
    seeds = jax.random.split(jax.random.key(seed), 10)
    return {
        "patches": scatter_about(seeds[0], (CLIPS, SLOTS, PATCH_DIM), 1.0, 6.0, ((0, 8), (1, 4))),
        "patch_index": with_ends(jax.random.randint(seeds[1], (CLIPS, SLOTS), 0, PATCHES), jax.random.fold_in(seeds[1], 1), 0, PATCHES - 1).astype(jnp.int32),
        "counts": jax.vmap(lambda own: uneven_parts(own, BINS, 3 * VIS_DEV * BINS // 4, VIS_DEV, 2))(jax.random.split(seeds[2], CLIPS)).reshape((CLIPS, BINS)).astype(jnp.int32),
        "w_embed": scatter_about(seeds[3], (PATCH_DIM, D), PATCH_DIM ** -0.5, 0.25),
        "embed_bias": scatter_about(seeds[4], (D,), 0.5, 3.0),
        "ln_gain": jnp.clip(1.0 + 0.18 * jax.random.normal(seeds[5], (D,), jnp.float32), 0.099609375, 1.8984375).astype(jnp.bfloat16),
        "w_qkv": draw_w_qkv(jax.random.fold_in(seeds[9], 71), 0),
        "w_o": scatter_about(seeds[7], (D, D), D ** -0.5, 0.1875, ((0, 4),)),
        "cotangent": scatter_about(seeds[8], (CLIPS, SLOTS, D), 1.0, 6.0, ((0, 8), (1, 4))),
    }


NEG_FILL = -1e+30
NORM_EPS = 1e-05

def sincos_features(coord, width):
    half_width = width // 2
    step_ids = jnp.arange(half_width).astype(jnp.float32)
    frequency = 10000.0 ** (-step_ids / half_width)
    phase = coord.astype(jnp.float32)[:, None] * frequency[None, :]
    return jnp.concatenate([jnp.sin(phase), jnp.cos(phase)], axis=1)

def position_table(patch_ids, bin_ids, width):
    time_width = width // 4
    space_width = (width - time_width) // 2
    return jnp.concatenate([sincos_features(bin_ids, time_width), sincos_features(patch_ids // PATCH_COLS, space_width), sincos_features(patch_ids % PATCH_COLS, space_width)], axis=1)

def layer_norm(rows_in, ln_gain):
    values = rows_in.astype(jnp.float32)
    row_mean = lax.optimization_barrier(jnp.mean(values, axis=-1, keepdims=True))
    centred = values - row_mean
    variance = lax.optimization_barrier(jnp.mean(centred * centred, axis=-1, keepdims=True))
    return (centred * lax.rsqrt(variance + NORM_EPS) * ln_gain.astype(jnp.float32)).astype(jnp.bfloat16)

def reference(patches, patch_index, counts, w_embed, embed_bias, ln_gain, w_qkv, w_o, cotangent):
    slot_ids = jnp.arange(SLOTS).astype(jnp.int32)
    bin_ids = slot_ids // VIS_DEV
    bin_table = bin_ids[:, None] == jnp.arange(BINS).astype(jnp.int32)[None, :]
    score_scale = 1.0 / math.sqrt(HEAD_DIM)

    def clip_step(grad_running, operands):
        clip_patches, clip_index, clip_counts, clip_cot = operands
        count_of = lax.optimization_barrier(jnp.sum(jnp.where(bin_table, clip_counts[None, :], 0), axis=1))
        valid_rows = slot_ids % VIS_DEV < count_of
        position = position_table(clip_index, bin_ids, D)
        embedded = jnp.dot(clip_patches, w_embed, preferred_element_type=jnp.float32)
        embedded = embedded + embed_bias.astype(jnp.float32) + position
        hidden_rows = jnp.where(valid_rows[:, None], embedded, 0.0).astype(jnp.bfloat16)
        normed = layer_norm(hidden_rows, ln_gain)
        qkv = jnp.dot(normed, w_qkv, preferred_element_type=jnp.float32).astype(jnp.bfloat16)
        qkv = qkv.reshape(SLOTS, HEADS, 3, HEAD_DIM).transpose(1, 2, 0, 3)

        def one_head(head_qkv):
            scores = jnp.dot(head_qkv[0], head_qkv[1].T, preferred_element_type=jnp.float32) * score_scale
            scores = jnp.where(valid_rows[None, :], scores, NEG_FILL)
            row_max = lax.optimization_barrier(jnp.max(scores, axis=1, keepdims=True))
            weights = jnp.exp(scores - row_max)
            weight_sum = lax.optimization_barrier(jnp.sum(weights, axis=1, keepdims=True))
            mixed = jnp.dot(weights.astype(jnp.bfloat16), head_qkv[2], preferred_element_type=jnp.float32)
            return (mixed / weight_sum).astype(jnp.bfloat16)
        attended = lax.map(one_head, qkv).transpose(1, 0, 2).reshape(SLOTS, D)
        projected = jnp.dot(attended, w_o, preferred_element_type=jnp.float32)
        encoded = jnp.where(valid_rows[:, None], hidden_rows.astype(jnp.float32) + projected, 0.0).astype(jnp.bfloat16)
        cot_rows = jnp.where(valid_rows[:, None], clip_cot, jnp.zeros((), jnp.bfloat16))
        grad_running = grad_running + jnp.dot(attended.T, cot_rows, preferred_element_type=jnp.float32)
        return (grad_running, encoded)
    grad_total, encoded = lax.scan(clip_step, jnp.zeros((D, D), jnp.float32), (patches, patch_index, counts, cotangent))
    grad_w_o = grad_total * (1.0 / math.sqrt(CLIPS * SLOTS))
    return (encoded, grad_w_o)
```

```python
import functools
import math

import jax
import jax.numpy as jnp
import ml_dtypes
import numpy as np
from jax import lax
from jax.experimental import pallas as pl
from jax.experimental.pallas import tpu as pltpu
from jax.sharding import PartitionSpec as P

HEAD_DIM = 64
PATCH_COLS = 80
PATCH_ROWS = 45
NEG_FILL = -1e30
NORM_EPS = 1e-05
VMEM_LIMIT = 50 * 1024 * 1024
F32 = jnp.float32
BF16 = jnp.bfloat16


def sincos_features(coord, width):
    half_width = width // 2
    step_ids = jnp.arange(half_width).astype(jnp.float32)
    frequency = 10000.0 ** (-step_ids / half_width)
    phase = coord.astype(jnp.float32)[:, None] * frequency[None, :]
    return jnp.concatenate([jnp.sin(phase), jnp.cos(phase)], axis=1)


def position_table(patch_ids, bin_ids, width):
    time_width = width // 4
    space_width = (width - time_width) // 2
    return jnp.concatenate(
        [
            sincos_features(bin_ids, time_width),
            sincos_features(patch_ids // PATCH_COLS, space_width),
            sincos_features(patch_ids % PATCH_COLS, space_width),
        ],
        axis=1,
    )


def layer_norm(rows_in, ln_gain):
    values = rows_in.astype(jnp.float32)
    row_mean = jnp.mean(values, axis=-1, keepdims=True)
    centred = values - row_mean
    variance = jnp.mean(centred * centred, axis=-1, keepdims=True)
    return (centred * lax.rsqrt(variance + NORM_EPS) * ln_gain.astype(jnp.float32)).astype(
        jnp.bfloat16
    )


def attend_heads(mixed_rows, key_valid):
    total_rows = mixed_rows.shape[0]
    heads_here = mixed_rows.shape[1] // (3 * HEAD_DIM)
    split_rows = mixed_rows.reshape(total_rows, heads_here, 3, HEAD_DIM)
    queries = split_rows[:, :, 0]
    keys_all = split_rows[:, :, 1]
    values_all = split_rows[:, :, 2]
    block_rows = math.gcd(total_rows, 512)
    query_blocks = queries.reshape(total_rows // block_rows, block_rows, heads_here, HEAD_DIM)
    score_scale = 1.0 / math.sqrt(HEAD_DIM)

    def one_block(query_block):
        scores = (
            jnp.einsum("qhd,khd->hqk", query_block, keys_all, preferred_element_type=jnp.float32)
            * score_scale
        )
        scores = jnp.where(key_valid[None, None, :], scores, NEG_FILL)
        row_max = jnp.max(scores, axis=2, keepdims=True)
        weights = jnp.exp(scores - row_max)
        weight_sum = jnp.sum(weights, axis=2, keepdims=True)
        mixed = jnp.einsum(
            "hqk,khd->qhd",
            weights.astype(jnp.bfloat16),
            values_all,
            preferred_element_type=jnp.float32,
        )
        return (mixed / weight_sum.transpose(1, 0, 2)).astype(jnp.bfloat16)

    outcome = lax.map(one_block, query_blocks)
    return outcome.reshape(total_rows, heads_here * HEAD_DIM)


def general_device(
    patches, patch_index, counts, w_embed, embed_bias, ln_gain, w_qkv, w_o, cotangent
):
    row_count = patches.shape[1]
    width = w_embed.shape[1]
    bin_total = lax.axis_size("tm")
    clip_total = lax.axis_size("clip")
    bin_now = lax.axis_index("tm")
    local_slots = jnp.arange(row_count)
    valid_rows = local_slots < counts[0, 0]
    bin_ids = jnp.zeros((row_count,), jnp.int32) + bin_now
    position = position_table(patch_index[0], bin_ids, width)
    embedded = jnp.dot(patches[0], w_embed, preferred_element_type=jnp.float32)
    embedded = embedded + embed_bias.astype(jnp.float32) + position
    hidden_rows = jnp.where(valid_rows[:, None], embedded, 0.0).astype(jnp.bfloat16)
    normed = layer_norm(hidden_rows, ln_gain)
    all_counts = lax.all_gather(counts, "tm", axis=1, tiled=True)
    key_slots = jnp.arange(row_count * bin_total)
    key_bins = key_slots // row_count
    bin_table = key_bins[:, None] == jnp.arange(bin_total)[None, :]
    key_count = jnp.sum(jnp.where(bin_table, all_counts[0][None, :], 0), axis=1)
    key_valid = key_slots % row_count < key_count
    mixed_rows = jnp.dot(
        lax.all_gather(normed, "tm", axis=0, tiled=True), w_qkv, preferred_element_type=jnp.float32
    ).astype(jnp.bfloat16)
    head_rows = attend_heads(mixed_rows, key_valid)
    attended = lax.all_to_all(head_rows, "tm", split_axis=0, concat_axis=1, tiled=True)
    projected = jnp.dot(
        attended, lax.all_gather(w_o, "tm", axis=0, tiled=True), preferred_element_type=jnp.float32
    )
    encoded = jnp.where(
        valid_rows[:, None], hidden_rows.astype(jnp.float32) + projected, 0.0
    ).astype(jnp.bfloat16)
    cot_rows = jnp.where(valid_rows[:, None], cotangent[0], jnp.zeros((), jnp.bfloat16))
    grad_scale = 1.0 / math.sqrt(clip_total * row_count * bin_total)
    grad_part = lax.psum_scatter(
        jnp.dot(attended.T, cot_rows, preferred_element_type=jnp.float32).astype(jnp.bfloat16),
        "tm",
        scatter_dimension=0,
        tiled=True,
    )
    grad_rows = lax.psum(grad_part, "clip").astype(jnp.float32)
    grad_w_o = grad_rows * grad_scale
    return (encoded[None], grad_w_o)


META = 16


def sincos_np(coord, width):
    half_width = width // 2
    frequency = 10000.0 ** (-np.arange(half_width) / half_width)
    phase = np.asarray(coord, np.float64)[:, None] * frequency[None, :]
    return np.concatenate([np.sin(phase), np.cos(phase)], axis=1)


def position_parts(bin_total, width):
    time_width = width // 4
    space_width = (width - time_width) // 2
    table = np.zeros((128, 2 * space_width), np.float64)
    table[:PATCH_ROWS, :space_width] = sincos_np(np.arange(PATCH_ROWS), space_width)
    table[PATCH_ROWS : PATCH_ROWS + PATCH_COLS, space_width:] = sincos_np(
        np.arange(PATCH_COLS), space_width
    )
    high = table.astype(ml_dtypes.bfloat16)
    low = (table - high.astype(np.float64)).astype(ml_dtypes.bfloat16)
    bins = np.zeros((8, time_width), np.float32)
    bins[:bin_total] = sincos_np(np.arange(bin_total), time_width)
    return np.concatenate([high, low], axis=0), bins


def vmem_call(kernel, out_shape, scalars, arrays, scratch=(), flops=0):
    n_scalar = len(scalars)
    specs = [pl.BlockSpec(memory_space=pltpu.SMEM)] * n_scalar
    specs += [pl.BlockSpec(memory_space=pltpu.VMEM)] * len(arrays)
    size = sum(math.prod(a.shape) * a.dtype.itemsize for a in arrays)
    return pl.pallas_call(
        kernel,
        out_shape=out_shape,
        in_specs=specs,
        out_specs=jax.tree.map(lambda _: pl.BlockSpec(memory_space=pltpu.VMEM), out_shape),
        scratch_shapes=list(scratch),
        compiler_params=pltpu.CompilerParams(vmem_limit_bytes=VMEM_LIMIT),
        cost_estimate=pl.CostEstimate(flops=flops, bytes_accessed=size, transcendentals=0),
    )(*scalars, *arrays)


def pack_kernel(clip_ref, count_ref, patch_ref, index_ref, w_ref, packet_ref, meta):
    rows = patch_ref.shape[0]
    half = patch_ref.shape[1]
    piece = w_ref.shape[0] // 8
    packet_ref[0:rows, :] = patch_ref[...]
    index = jnp.clip(index_ref[...], 0, PATCH_ROWS * PATCH_COLS - 1).astype(F32)
    patch_row = jnp.floor((index + 0.5) * (1.0 / PATCH_COLS))
    meta[...] = jnp.full(meta.shape, 1.0, F32) * count_ref[0].astype(F32)
    meta[0:1, 0:rows] = patch_row
    meta[0:1, 256 : 256 + rows] = index - patch_row * PATCH_COLS
    packet_ref[rows : rows + META, :] = meta[...].astype(BF16)
    start = pl.multiple_of(clip_ref[0] * piece, piece)
    base = rows + META
    packet_ref[base : base + piece, :] = w_ref[pl.ds(start, piece), 0:half]
    packet_ref[base + piece : base + 2 * piece, :] = w_ref[pl.ds(start, piece), half : 2 * half]


def attend_kernel(
    rows,
    bin_ref,
    p0_ref,
    p1_ref,
    p2_ref,
    pb_ref,
    pf_ref,
    w_embed_ref,
    table_ref,
    bins_ref,
    bias_ref,
    gain_ref,
    w_qkv_ref,
    a0_ref,
    a1_ref,
    a2_ref,
    a3_ref,
    hidden_ref,
    piece_ref,
    p3_ref,
    q_ref,
    k_ref,
    v_ref,
):
    me = bin_ref[0]
    inner = jnp.logical_or(me == 1, me == 2)

    @pl.when(inner)
    def _():
        p3_ref[...] = pb_ref[...]

    @pl.when(jnp.logical_not(inner))
    def _():
        p3_ref[...] = pf_ref[...]

    packets = (p0_ref, p1_ref, p2_ref, p3_ref)
    outs = (a0_ref, a1_ref, a2_ref, a3_ref)
    group = 4 * HEAD_DIM
    slot = lax.broadcasted_iota(jnp.int32, (rows, 1), 0).astype(F32)
    place = lax.broadcasted_iota(jnp.int32, (128, rows), 0).astype(F32)
    bias = bias_ref[...].astype(F32)
    gain = gain_ref[...].astype(F32)
    valid = []
    for k in range(4):
        packet = packets[k]
        base = rows + META
        piece_ref[k] = packet[base:, :]
        meta = packet[rows : rows + META, :].astype(F32)
        count = meta[1:2, 0:1]
        ok = slot < count
        valid.append(ok)
        hit = jnp.logical_or(
            place == meta[0:1, 0:rows], place == meta[0:1, 256 : 256 + rows] + PATCH_ROWS
        )
        hot = jnp.where(hit, 1.0, 0.0).astype(BF16)
        hot = jnp.concatenate([hot, hot], axis=0)
        space = lax.dot_general(
            hot, table_ref[...], (((0,), (0,)), ((), ())), preferred_element_type=F32
        )
        embedded = jnp.dot(packet[0:rows, :], w_embed_ref[...], preferred_element_type=F32)
        times = bins_ref[pl.ds(jnp.bitwise_xor(me, k), 1), :]
        times = jnp.broadcast_to(times, (rows, times.shape[1]))
        embedded = embedded + bias + jnp.concatenate([times, space], axis=1)
        hidden = jnp.where(ok, embedded, 0.0).astype(BF16)
        if k == 0:
            hidden_ref[...] = hidden
        values = hidden.astype(F32)
        centred = values - jnp.mean(values, axis=1, keepdims=True)
        variance = jnp.mean(centred * centred, axis=1, keepdims=True)
        normed = (centred * lax.rsqrt(variance + NORM_EPS) * gain).astype(BF16)
        qkv = jnp.dot(normed, w_qkv_ref[...], preferred_element_type=F32).astype(BF16)
        here = slice(k * rows, (k + 1) * rows)
        q_ref[here, :] = qkv[:, 0:group] * jnp.asarray(1.0 / math.sqrt(HEAD_DIM), BF16)
        k_ref[here, :] = qkv[:, group : 2 * group]
        v_ref[here, :] = qkv[:, 2 * group : 3 * group]

    lane = lax.broadcasted_iota(jnp.int32, (1, group), 1)
    key_bias = jnp.concatenate([jnp.where(ok, 0.0, NEG_FILL) for ok in valid], axis=0)
    total = [None] * 4
    for h in range(4):
        own = jnp.logical_and(lane >= h * HEAD_DIM, lane < (h + 1) * HEAD_DIM)
        spare_at = ((h + 1) * HEAD_DIM) % group
        spare = lane == spare_at
        keys = jnp.where(own, k_ref[...].astype(F32), jnp.where(spare, key_bias, 0.0)).astype(BF16)
        rest = jnp.where(spare, 1.0, 0.0)
        vals = jnp.where(own, v_ref[...].astype(F32), rest).astype(BF16)
        for b in range(4):
            queries = q_ref[b * rows : (b + 1) * rows, :].astype(F32)
            queries = jnp.where(own, queries, rest).astype(BF16)
            scores = lax.dot_general(
                queries, keys, (((1,), (1,)), ((), ())), preferred_element_type=F32
            )
            weights = jnp.exp(scores - jnp.max(scores, axis=1, keepdims=True)).astype(BF16)
            mixed = jnp.dot(weights, vals, preferred_element_type=F32)
            mixed = mixed / mixed[:, spare_at : spare_at + 1]
            total[b] = mixed if h == 0 else jnp.where(own, mixed, total[b])
    for b in range(4):
        outs[b][...] = jnp.where(valid[b], total[b], 0.0).astype(BF16)


def grad_kernel(
    bin_ref,
    core_ref,
    a0_ref,
    a1_ref,
    a2_ref,
    a3_ref,
    c0_ref,
    c1_ref,
    c2_ref,
    cb_ref,
    cf_ref,
    keep_ref,
    send_ref,
    c3_ref,
    sum_ref,
):
    me = bin_ref[0]
    inner = jnp.logical_or(me == 1, me == 2)

    @pl.when(inner)
    def _():
        c3_ref[...] = cb_ref[...]

    @pl.when(jnp.logical_not(inner))
    def _():
        c3_ref[...] = cf_ref[...]

    total = None
    for a_ref, c_ref in ((a0_ref, c0_ref), (a1_ref, c1_ref), (a2_ref, c2_ref), (a3_ref, c3_ref)):
        part = lax.dot_general(
            a_ref[...], c_ref[...], (((0,), (0,)), ((), ())), preferred_element_type=F32
        )
        total = part if total is None else total + part
    sum_ref[...] = total
    half = sum_ref.shape[0] // 2
    core = core_ref[0]
    keep_ref[...] = sum_ref[pl.ds(pl.multiple_of(core * half, half), half), :].astype(BF16)
    send_ref[...] = sum_ref[pl.ds(pl.multiple_of((1 - core) * half, half), half), :].astype(BF16)


def gather_kernel(clip_ref, *refs):
    out_ref = refs[-1]
    clip = clip_ref[0]
    piece = refs[0].shape[1] // 2
    half = refs[0].shape[2]
    for m in range(8):
        start = pl.multiple_of(jnp.bitwise_xor(clip, m) * piece, piece)
        for k in range(4):
            out_ref[k, pl.ds(start, piece), 0:half] = refs[m][k, 0:piece, :]
            out_ref[k, pl.ds(start, piece), half : 2 * half] = refs[m][k, piece : 2 * piece, :]


def project_kernel(count_ref, hidden_ref, a0_ref, a1_ref, a2_ref, a3_ref, w_ref, out_ref):
    rows = hidden_ref.shape[0]
    heads = jnp.concatenate([a0_ref[...], a1_ref[...], a2_ref[...], a3_ref[...]], axis=1)
    slot = lax.broadcasted_iota(jnp.int32, (rows, 1), 0)
    projected = jnp.dot(heads, w_ref[...], preferred_element_type=F32)
    total = hidden_ref[...].astype(F32) + projected
    out_ref[...] = jnp.where(slot < count_ref[0], total, 0.0).astype(BF16)


def finish_kernel(scale, core_ref, *refs):
    out_ref = refs[-1]
    core = core_ref[0]
    half = out_ref.shape[0] // 2
    parts = (len(refs) - 1) // 3
    width = out_ref.shape[1] // parts
    for c in range(parts):
        upper, lower, other = refs[3 * c : 3 * c + 3]
        columns = slice(c * width, (c + 1) * width)
        quarter = half // 2
        mine = pl.multiple_of(core * half, half)
        theirs = pl.multiple_of((1 - core) * half, half)
        out_ref[pl.ds(mine, quarter), columns] = upper[...].astype(F32) * scale
        out_ref[pl.ds(mine + quarter, quarter), columns] = lower[...].astype(F32) * scale
        out_ref[pl.ds(theirs, half), columns] = other[...].astype(F32) * scale


def along_tm(array, pairs):
    return lax.ppermute(array, "tm", pairs)


def along_clip(array, flip):
    return lax.ppermute(array, "clip", [(i, i ^ flip) for i in range(8)])


NEAR = [(0, 1), (1, 0), (2, 3), (3, 2)]
MIDDLE = [(1, 2), (2, 1)]
TWO = [(0, 2), (1, 3), (2, 0), (3, 1)]
RELAY = [(2, 3), (1, 0)]


def add_rounded(first, second):
    return (first.astype(F32) + second.astype(F32)).astype(BF16)


def after(value, *others):
    return lax.optimization_barrier((value, *others))[0]


def line_device(
    patches, patch_index, counts, w_embed, embed_bias, ln_gain, w_qkv, w_o, cotangent
):
    rows = patches.shape[1]
    half = patches.shape[2]
    width = w_embed.shape[1]
    group = 4 * HEAD_DIM
    piece = w_o.shape[0] // 8
    me = lax.axis_index("tm").astype(jnp.int32)
    clip = lax.axis_index("clip").astype(jnp.int32)
    core = clip % 2
    me_s, clip_s, core_s = me[None], clip[None], core[None]
    count_s = counts[0]
    shape = jax.ShapeDtypeStruct
    table, bins = position_parts(4, width)

    packet = vmem_call(
        pack_kernel,
        shape((rows + META + 2 * piece, half), BF16),
        [clip_s, count_s],
        [patches[0], patch_index, w_o],
        scratch=[pltpu.VMEM((META, half), F32)],
    )
    cots = [cotangent[0][:, :half], cotangent[0][:, half:]]

    def send(array):
        near = along_tm(array, NEAR)
        two = along_tm(array, TWO)
        middle = along_tm(array, MIDDLE)
        return near, two, middle

    p1, p2, pb = send(packet)
    c1, c2, cb = send(after(cots[0], p1))
    pf = along_tm(p2, RELAY)
    d1, d2, db = send(after(cots[1], c1))
    cf = along_tm(c2, RELAY)
    df = along_tm(d2, RELAY)

    w_ordered = w_qkv.reshape(width, 4, 3, HEAD_DIM).transpose(0, 2, 1, 3).reshape(width, 3 * group)
    a_shape = shape((rows, group), BF16)
    *heads, hidden, pieces = vmem_call(
        functools.partial(attend_kernel, rows),
        [a_shape] * 4 + [shape((rows, width), BF16), shape((4, 2 * piece, half), BF16)],
        [me_s],
        [
            packet,
            p1,
            p2,
            pb,
            pf,
            w_embed,
            jnp.asarray(table),
            jnp.asarray(bins),
            embed_bias[None],
            ln_gain[None],
            w_ordered,
        ],
        scratch=[pltpu.VMEM(packet.shape, BF16)] + [pltpu.VMEM((4 * rows, group), BF16)] * 3,
        flops=4_000_000_000,
    )

    by_x = along_clip(pieces, 2)
    by_y = along_clip(pieces, 4)
    onward = jnp.where(core == 0, by_x, by_y)
    turn = [(i, i ^ 4) if i % 2 == 0 else (i, i ^ 2) for i in range(8)]
    by_xy = lax.ppermute(onward, "clip", turn)
    held = {0: pieces, 2: by_x, 4: by_y, 6: by_xy}
    for m in (0, 2, 4, 6):
        held[m + 1] = along_clip(held[m], 1)
    w_all = vmem_call(
        gather_kernel,
        shape((4, 8 * piece, width), BF16),
        [clip_s],
        [held[m] for m in range(8)],
    ).reshape(width, width)

    finals = []
    for own, one, two, mid, far in (
        (cots[0], c1, c2, cb, cf),
        (cots[1], d1, d2, db, df),
    ):
        keep, give = vmem_call(
            grad_kernel,
            [shape((group // 2, half), BF16)] * 2,
            [me_s, core_s],
            [*heads, own, one, two, mid, far],
            scratch=[pltpu.VMEM((rows, half), BF16), pltpu.VMEM((group, half), F32)],
            flops=400_000_000,
        )
        mine = add_rounded(keep, along_clip(give, 1))
        quarter = group // 4
        upper, lower = mine[:quarter], mine[quarter:]
        upper, lower = (
            add_rounded(upper, along_clip(upper, 2)),
            add_rounded(lower, along_clip(lower, 4)),
        )
        upper, lower = (
            add_rounded(upper, along_clip(upper, 4)),
            add_rounded(lower, along_clip(lower, 2)),
        )
        other = along_clip(jnp.concatenate([upper, lower], axis=0), 1)
        finals += [upper, lower, other]

    moved = [heads[0]]
    for k in (1, 2, 3):
        block = after(heads[k], df)
        moved.append(along_tm(block, [(i, i ^ k) for i in range(4)]))
    encoded = vmem_call(
        project_kernel,
        shape((rows, width), BF16),
        [count_s],
        [hidden, *moved, w_all],
        flops=400_000_000,
    )
    grad_w_o = vmem_call(
        functools.partial(finish_kernel, 1.0 / math.sqrt(8 * rows * 4)),
        shape((group, width), F32),
        [core_s],
        finals,
    )
    return (encoded[None], grad_w_o)


def solution(mesh):
    in_specs = (
        P("clip", "tm", None),
        P("clip", "tm"),
        P("clip", "tm"),
        P(),
        P(),
        P(),
        P(None, "tm"),
        P("tm", None),
        P("clip", "tm", None),
    )
    out_specs = (P("clip", "tm", None), P("tm", None))
    on_line = mesh.shape["tm"] == 4 and mesh.shape["clip"] == 8
    return jax.shard_map(
        line_device if on_line else general_device,
        mesh=mesh,
        in_specs=in_specs,
        out_specs=out_specs,
        check_vma=False,
    )
```

```python
import functools
import math

import jax
import jax.numpy as jnp
import ml_dtypes
import numpy as np
from jax import lax
from jax.experimental import pallas as pl
from jax.experimental.pallas import tpu as pltpu
from jax.sharding import PartitionSpec as P

HEAD_DIM = 64
PATCH_COLS = 80
PATCH_ROWS = 45
NEG_FILL = -1e30
NORM_EPS = 1e-05
F32 = jnp.float32
BF16 = jnp.bfloat16


def sincos_features(coord, width):
    half_width = width // 2
    step_ids = jnp.arange(half_width).astype(jnp.float32)
    frequency = 10000.0 ** (-step_ids / half_width)
    phase = coord.astype(jnp.float32)[:, None] * frequency[None, :]
    return jnp.concatenate([jnp.sin(phase), jnp.cos(phase)], axis=1)


def position_table(patch_ids, bin_ids, width):
    time_width = width // 4
    space_width = (width - time_width) // 2
    return jnp.concatenate(
        [
            sincos_features(bin_ids, time_width),
            sincos_features(patch_ids // PATCH_COLS, space_width),
            sincos_features(patch_ids % PATCH_COLS, space_width),
        ],
        axis=1,
    )


def layer_norm(rows_in, ln_gain):
    values = rows_in.astype(jnp.float32)
    row_mean = jnp.mean(values, axis=-1, keepdims=True)
    centred = values - row_mean
    variance = jnp.mean(centred * centred, axis=-1, keepdims=True)
    return (centred * lax.rsqrt(variance + NORM_EPS) * ln_gain.astype(jnp.float32)).astype(
        jnp.bfloat16
    )


def attend_heads(mixed_rows, key_valid):
    total_rows = mixed_rows.shape[0]
    heads_here = mixed_rows.shape[1] // (3 * HEAD_DIM)
    split_rows = mixed_rows.reshape(total_rows, heads_here, 3, HEAD_DIM)
    queries = split_rows[:, :, 0]
    keys_all = split_rows[:, :, 1]
    values_all = split_rows[:, :, 2]
    block_rows = math.gcd(total_rows, 512)
    query_blocks = queries.reshape(total_rows // block_rows, block_rows, heads_here, HEAD_DIM)
    score_scale = 1.0 / math.sqrt(HEAD_DIM)

    def one_block(query_block):
        scores = (
            jnp.einsum("qhd,khd->hqk", query_block, keys_all, preferred_element_type=jnp.float32)
            * score_scale
        )
        scores = jnp.where(key_valid[None, None, :], scores, NEG_FILL)
        row_max = jnp.max(scores, axis=2, keepdims=True)
        weights = jnp.exp(scores - row_max)
        weight_sum = jnp.sum(weights, axis=2, keepdims=True)
        mixed = jnp.einsum(
            "hqk,khd->qhd",
            weights.astype(jnp.bfloat16),
            values_all,
            preferred_element_type=jnp.float32,
        )
        return (mixed / weight_sum.transpose(1, 0, 2)).astype(jnp.bfloat16)

    outcome = lax.map(one_block, query_blocks)
    return outcome.reshape(total_rows, heads_here * HEAD_DIM)


def general_device(
    patches, patch_index, counts, w_embed, embed_bias, ln_gain, w_qkv, w_o, cotangent
):
    row_count = patches.shape[1]
    width = w_embed.shape[1]
    bin_total = lax.axis_size("tm")
    clip_total = lax.axis_size("clip")
    bin_now = lax.axis_index("tm")
    local_slots = jnp.arange(row_count)
    valid_rows = local_slots < counts[0, 0]
    bin_ids = jnp.zeros((row_count,), jnp.int32) + bin_now
    position = position_table(patch_index[0], bin_ids, width)
    embedded = jnp.dot(patches[0], w_embed, preferred_element_type=jnp.float32)
    embedded = embedded + embed_bias.astype(jnp.float32) + position
    hidden_rows = jnp.where(valid_rows[:, None], embedded, 0.0).astype(jnp.bfloat16)
    normed = layer_norm(hidden_rows, ln_gain)
    all_counts = lax.all_gather(counts, "tm", axis=1, tiled=True)
    key_slots = jnp.arange(row_count * bin_total)
    key_bins = key_slots // row_count
    bin_table = key_bins[:, None] == jnp.arange(bin_total)[None, :]
    key_count = jnp.sum(jnp.where(bin_table, all_counts[0][None, :], 0), axis=1)
    key_valid = key_slots % row_count < key_count
    mixed_rows = jnp.dot(
        lax.all_gather(normed, "tm", axis=0, tiled=True), w_qkv, preferred_element_type=jnp.float32
    ).astype(jnp.bfloat16)
    head_rows = attend_heads(mixed_rows, key_valid)
    attended = lax.all_to_all(head_rows, "tm", split_axis=0, concat_axis=1, tiled=True)
    projected = jnp.dot(
        attended, lax.all_gather(w_o, "tm", axis=0, tiled=True), preferred_element_type=jnp.float32
    )
    encoded = jnp.where(
        valid_rows[:, None], hidden_rows.astype(jnp.float32) + projected, 0.0
    ).astype(jnp.bfloat16)
    cot_rows = jnp.where(valid_rows[:, None], cotangent[0], jnp.zeros((), jnp.bfloat16))
    grad_scale = 1.0 / math.sqrt(clip_total * row_count * bin_total)
    grad_part = lax.psum_scatter(
        jnp.dot(attended.T, cot_rows, preferred_element_type=jnp.float32).astype(jnp.bfloat16),
        "tm",
        scatter_dimension=0,
        tiled=True,
    )
    grad_rows = lax.psum(grad_part, "clip").astype(jnp.float32)
    grad_w_o = grad_rows * grad_scale
    return (encoded[None], grad_w_o)


META = 16


def sincos_np(coord, width):
    half_width = width // 2
    frequency = 10000.0 ** (-np.arange(half_width) / half_width)
    phase = np.asarray(coord, np.float64)[:, None] * frequency[None, :]
    return np.concatenate([np.sin(phase), np.cos(phase)], axis=1)


def position_parts(bin_total, width):
    time_width = width // 4
    space_width = (width - time_width) // 2
    table = np.zeros((128, 2 * space_width), np.float64)
    table[:PATCH_ROWS, :space_width] = sincos_np(np.arange(PATCH_ROWS), space_width)
    table[PATCH_ROWS : PATCH_ROWS + PATCH_COLS, space_width:] = sincos_np(
        np.arange(PATCH_COLS), space_width
    )
    high = table.astype(ml_dtypes.bfloat16)
    low = (table - high.astype(np.float64)).astype(ml_dtypes.bfloat16)
    bins = np.zeros((8, time_width), np.float32)
    bins[:bin_total] = sincos_np(np.arange(bin_total), time_width)
    return np.concatenate([high, low], axis=0), bins


def local_call(kernel, out_shape, scalars, arrays, spaces, out_spaces, scratch=(), limit=16, cost=1000):
    specs = [pl.BlockSpec(memory_space=pltpu.SMEM)] * len(scalars)
    specs += [pl.BlockSpec(memory_space=space) for space in spaces]
    return pl.pallas_call(
        kernel,
        out_shape=out_shape,
        in_specs=specs,
        out_specs=[pl.BlockSpec(memory_space=space) for space in out_spaces],
        scratch_shapes=list(scratch),
        compiler_params=pltpu.CompilerParams(vmem_limit_bytes=limit * 1024 * 1024),
        cost_estimate=pl.CostEstimate(flops=1000, bytes_accessed=cost, transcendentals=0),
    )(*scalars, *arrays)


VMEM, HBM = pltpu.VMEM, pltpu.HBM


def pack_kernel(count_ref, patch_ref, index_ref, packet_ref, meta):
    rows = patch_ref.shape[0]
    packet_ref[0:rows, :] = patch_ref[...]
    numbers = jnp.clip(index_ref[...], 0, PATCH_ROWS * PATCH_COLS - 1).astype(F32)
    patch_row = jnp.floor((numbers + 0.5) * (1.0 / PATCH_COLS))
    meta[...] = jnp.full(meta.shape, 1.0, F32) * count_ref[0].astype(F32)
    meta[0:1, 0:rows] = patch_row
    meta[0:1, 256 : 256 + rows] = numbers - patch_row * PATCH_COLS
    packet_ref[rows:, :] = meta[...].astype(BF16)


def halve_kernel(clip_ref, cot_ref, w_ref, first_ref, second_ref):
    rows = cot_ref.shape[0]
    half = first_ref.shape[1]
    piece = w_ref.shape[0] // 8
    start = pl.multiple_of(clip_ref[0] * piece, piece)
    first_ref[0:rows, :] = cot_ref[:, 0:half]
    first_ref[rows : rows + piece, :] = w_ref[pl.ds(start, piece), 0:half]
    first_ref[rows + piece :, :] = w_ref[pl.ds(start, piece), half : 2 * half]
    second_ref[...] = cot_ref[:, half : 2 * half]


def split_kernel(*refs):
    sources, piece_ref, sems = refs[:4], refs[4], refs[5]
    rows = sources[0].shape[0] - piece_ref.shape[1]
    copies = [
        pltpu.make_async_copy(source.at[rows:], piece_ref.at[k], sems.at[k])
        for k, source in enumerate(sources)
    ]
    for copy in copies:
        copy.start()
    for copy in copies:
        copy.wait()


def stage_kernel(w_qkv_ref, qkv_out):
    for part in range(3):
        for pair in range(2):
            first = (2 * pair * 3 + part) * HEAD_DIM
            second = first + 3 * HEAD_DIM
            both = jnp.concatenate(
                [
                    w_qkv_ref[:, first : first + HEAD_DIM],
                    w_qkv_ref[:, second : second + HEAD_DIM],
                ],
                axis=1,
            )
            at = (2 * part + pair) * 2 * HEAD_DIM
            qkv_out[:, at : at + 2 * HEAD_DIM] = both


def attend_kernel(
    rows,
    bin_ref,
    p0_hbm,
    p1_hbm,
    p2_hbm,
    p3_hbm,
    w_embed_hbm,
    table_hbm,
    bins_hbm,
    bias_hbm,
    gain_hbm,
    w_qkv_hbm,
    a_ref,
    a1_ref,
    a2_ref,
    a3_ref,
    hidden_ref,
    packets,
    w_embed_ref,
    table_ref,
    bins_ref,
    bias_ref,
    gain_ref,
    w_qkv_ref,
    normed_ref,
    q_ref,
    k_ref,
    v_ref,
    sems,
):
    me = bin_ref[0]
    copies = [
        pltpu.make_async_copy(source, packets.at[k], sems.at[k])
        for k, source in enumerate((p0_hbm, p1_hbm, p2_hbm, p3_hbm))
    ]
    for copy in copies:
        copy.start()
    staged = [
        pltpu.make_async_copy(source, target, sems.at[4 + i])
        for i, (source, target) in enumerate(
            (
                (w_embed_hbm, w_embed_ref),
                (table_hbm, table_ref),
                (bins_hbm, bins_ref),
                (bias_hbm, bias_ref),
                (gain_hbm, gain_ref),
                (w_qkv_hbm, w_qkv_ref),
            )
        )
    ]
    for copy in staged:
        copy.start()
    for copy in copies:
        copy.wait()
    for copy in staged[:-1]:
        copy.wait()
    group = 4 * HEAD_DIM
    slot = lax.broadcasted_iota(jnp.int32, (rows, 1), 0).astype(F32)
    place = lax.broadcasted_iota(jnp.int32, (128, rows), 0).astype(F32)
    lane = lax.broadcasted_iota(jnp.int32, (1, group), 1)
    bias = bias_ref[...].astype(F32)
    gain = gain_ref[...].astype(F32)
    owns, spares, spare_at = [], [], []
    for h in range(4):
        own = jnp.logical_and(lane >= h * HEAD_DIM, lane < (h + 1) * HEAD_DIM)
        spare_at.append((h * HEAD_DIM + group // 2) % group)
        owns.append(jnp.where(own, 1.0, 0.0).astype(BF16))
        spares.append(jnp.where(lane == spare_at[h], 1.0, 0.0))
    valid = []
    for k in range(4):
        here = slice(k * rows, (k + 1) * rows)
        meta = packets[k, rows:, :].astype(F32)
        ok = slot < meta[1:2, 0:1]
        valid.append(ok)
        hit = jnp.logical_or(
            place == meta[0:1, 0:rows], place == meta[0:1, 256 : 256 + rows] + PATCH_ROWS
        )
        hot = jnp.where(hit, 1.0, 0.0).astype(BF16)
        hot = jnp.concatenate([hot, hot], axis=0)
        space = lax.dot_general(
            hot, table_ref[...], (((0,), (0,)), ((), ())), preferred_element_type=F32
        )
        embedded = jnp.dot(packets[k, 0:rows, :], w_embed_ref[...], preferred_element_type=F32)
        times = bins_ref[pl.ds(jnp.bitwise_xor(me, k), 1), :]
        times = jnp.broadcast_to(times, (rows, times.shape[1]))
        embedded = embedded + bias + jnp.concatenate([times, space], axis=1)
        hidden = jnp.where(ok, embedded, 0.0).astype(BF16)
        if k == 0:
            hidden_ref[...] = hidden
        values = hidden.astype(F32)
        centred = values - jnp.mean(values, axis=1, keepdims=True)
        variance = jnp.mean(centred * centred, axis=1, keepdims=True)
        normed_ref[here, :] = (centred * lax.rsqrt(variance + NORM_EPS) * gain).astype(BF16)
    mask = jnp.concatenate([jnp.where(ok, 0.0, NEG_FILL) for ok in valid], axis=0)
    staged[-1].wait()
    for part, ref in enumerate((q_ref, k_ref, v_ref)):
        mixed = jnp.dot(
            normed_ref[...],
            w_qkv_ref[:, part * group : (part + 1) * group],
            preferred_element_type=F32,
        ).astype(BF16)
        if part == 0:
            mixed = mixed * jnp.asarray(1.0 / math.sqrt(HEAD_DIM), BF16)
        for h in range(4):
            fill = (mask * spares[h]).astype(BF16) if part == 1 else spares[h].astype(BF16)
            ref[h] = mixed * owns[h] + fill

    total = None
    for h in range(4):
        scores = lax.dot_general(
            q_ref[h], k_ref[h], (((1,), (1,)), ((), ())), preferred_element_type=F32
        )
        weights = jnp.exp(scores - jnp.max(scores, axis=1, keepdims=True)).astype(BF16)
        mixed = jnp.dot(weights, v_ref[h], preferred_element_type=F32)
        mixed = mixed * (1.0 / mixed[:, spare_at[h] : spare_at[h] + 1])
        total = mixed if h == 0 else jnp.where(owns[h] > 0, mixed, total)
    total = jnp.where(mask == 0.0, total, 0.0).astype(BF16)
    a_ref[...] = total
    for k, ref in enumerate((a1_ref, a2_ref, a3_ref)):
        ref[...] = total[(k + 1) * rows : (k + 2) * rows, :]


def grad_kernel(
    core_ref, a_ref, c0_hbm, c1_hbm, c2_hbm, c3_hbm, keep_ref, send_ref, cots, sum_ref, sems
):
    rows = cots.shape[0] // 4
    copies = [
        pltpu.make_async_copy(source.at[0:rows], cots.at[pl.ds(k * rows, rows)], sems.at[k])
        for k, source in enumerate((c0_hbm, c1_hbm, c2_hbm, c3_hbm))
    ]
    for copy in copies:
        copy.start()
    for copy in copies:
        copy.wait()
    sum_ref[...] = lax.dot_general(
        a_ref[...], cots[...], (((0,), (0,)), ((), ())), preferred_element_type=F32
    )
    half = sum_ref.shape[0] // 2
    core = core_ref[0]
    keep_ref[...] = sum_ref[pl.ds(pl.multiple_of(core * half, half), half), :].astype(BF16)
    send_ref[...] = sum_ref[pl.ds(pl.multiple_of((1 - core) * half, half), half), :].astype(BF16)


def gather_kernel(clip_ref, *refs):
    held, out_hbm, sems = refs[:8], refs[8], refs[9]
    clip = clip_ref[0]
    piece = held[0].shape[1] // 2
    half = held[0].shape[2]
    copies = []
    for m in range(8):
        start = pl.multiple_of(jnp.bitwise_xor(clip, m) * piece, piece)
        for k in range(4):
            for side in range(2):
                copies.append(
                    pltpu.make_async_copy(
                        held[m].at[k, side * piece : (side + 1) * piece],
                        out_hbm.at[k, pl.ds(start, piece), side * half : (side + 1) * half],
                        sems.at[len(copies)],
                    )
                )
                copies[-1].start()
    for copy in copies:
        copy.wait()


def project_kernel(
    count_ref, hidden_hbm, a0_hbm, a1_hbm, a2_hbm, a3_hbm, w_hbm, out_hbm, hidden, heads, w_all, out, sems
):
    rows, group = a1_hbm.shape
    copies = [
        pltpu.make_async_copy(w_hbm, w_all, sems.at[0]),
        pltpu.make_async_copy(hidden_hbm, hidden, sems.at[1]),
        pltpu.make_async_copy(a0_hbm.at[0:rows], heads.at[:, 0:group], sems.at[2]),
    ]
    for k, source in enumerate((a1_hbm, a2_hbm, a3_hbm)):
        columns = slice((k + 1) * group, (k + 2) * group)
        copies.append(pltpu.make_async_copy(source, heads.at[:, columns], sems.at[3 + k]))
    for copy in copies:
        copy.start()
    for copy in copies:
        copy.wait()
    slot = lax.broadcasted_iota(jnp.int32, (rows, 1), 0)
    projected = jnp.dot(heads[...], w_all[...], preferred_element_type=F32)
    total = hidden[...].astype(F32) + projected
    out[...] = jnp.where(slot < count_ref[0], total, 0.0).astype(BF16)
    write = pltpu.make_async_copy(out, out_hbm, sems.at[0])
    write.start()
    write.wait()


def finish_kernel(scale, core_ref, *refs):
    out_ref = refs[-1]
    core = core_ref[0]
    half = out_ref.shape[0] // 2
    parts = (len(refs) - 1) // 2
    width = out_ref.shape[1] // parts
    mine = pl.multiple_of(core * half, half)
    theirs = pl.multiple_of((1 - core) * half, half)
    for c in range(parts):
        columns = slice(c * width, (c + 1) * width)
        out_ref[pl.ds(mine, half), columns] = refs[2 * c][...].astype(F32) * scale
        out_ref[pl.ds(theirs, half), columns] = refs[2 * c + 1][...].astype(F32) * scale


def along_tm(array, flip):
    return lax.ppermute(array, "tm", [(i, i ^ flip) for i in range(4)])


def along_clip(array, flip):
    return lax.ppermute(array, "clip", [(i, i ^ flip) for i in range(8)])


def add_rounded(first, second):
    return (first.astype(F32) + second.astype(F32)).astype(BF16)


def after(value, *others):
    return lax.optimization_barrier((value, *others))[0]


def line_device(
    patches, patch_index, counts, w_embed, embed_bias, ln_gain, w_qkv, w_o, cotangent
):
    rows = patches.shape[1]
    half = patches.shape[2]
    width = w_embed.shape[1]
    group = 4 * HEAD_DIM
    piece = w_o.shape[0] // 8
    me = lax.axis_index("tm").astype(jnp.int32)
    clip = lax.axis_index("clip").astype(jnp.int32)
    core = clip % 2
    me_s, clip_s, core_s = me[None], clip[None], core[None]
    count_s = counts[0]
    shape = jax.ShapeDtypeStruct
    table, bins = position_parts(4, width)
    cot = cotangent[0]
    dma = pltpu.SemaphoreType.DMA

    (packet,) = local_call(
        pack_kernel,
        [shape((rows + META, half), BF16)],
        [count_s],
        [patches[0], patch_index],
        [VMEM] * 2,
        [VMEM],
        scratch=[VMEM((META, half), F32)],
        limit=4,
    )
    p1, p2, p3 = [along_tm(packet, k) for k in (1, 2, 3)]
    first, second = local_call(
        halve_kernel,
        [shape((rows + 2 * piece, half), BF16), shape((rows, half), BF16)],
        [clip_s],
        [cot, w_o],
        [VMEM] * 2,
        [VMEM] * 2,
        limit=4,
    )
    (w_ordered,) = local_call(
        stage_kernel, [shape((width, 3 * group), BF16)], [], [w_qkv], [VMEM], [VMEM], limit=8
    )
    bias_row, gain_row = embed_bias[None], ln_gain[None]
    c1 = along_tm(after(first, p1, w_ordered, bias_row, gain_row), 1)
    late = after(first, p1, p2, p3)
    c2, c3 = along_tm(late, 2), along_tm(late, 3)
    weights = [w_embed, jnp.asarray(table), jnp.asarray(bins), bias_row, gain_row]
    heads, *blocks, hidden = attend_call(
        me_s, [packet, p1, p2, after(p3, w_ordered, first)], [*weights, w_ordered], rows, width
    )
    d1 = along_tm(after(second, c1), 1)
    late = after(second, heads)
    d2, d3 = along_tm(late, 2), along_tm(late, 3)

    (pieces,) = local_call(
        split_kernel,
        [shape((4, 2 * piece, half), BF16)],
        [],
        [first, c1, c2, c3],
        [HBM] * 4,
        [VMEM],
        scratch=[dma((4,))],
        limit=4,
    )
    by_x = along_clip(pieces, 2)
    by_y = along_clip(pieces, 4)
    onward = jnp.where(core == 0, by_x, by_y)
    turn = [(i, i ^ 4) if i % 2 == 0 else (i, i ^ 2) for i in range(8)]
    by_xy = lax.ppermute(onward, "clip", turn)
    held = {0: pieces, 2: by_x, 4: by_y, 6: by_xy}
    for m in (0, 2, 4, 6):
        held[m + 1] = along_clip(held[m], 1)
    (w_all,) = local_call(
        gather_kernel,
        [shape((4, 8 * piece, width), BF16)],
        [clip_s],
        [held[m] for m in range(8)],
        [HBM] * 8,
        [HBM],
        scratch=[dma((64,))],
        limit=4,
    )
    w_all = w_all.reshape(width, width)

    moved = [heads]
    for k in (1, 2, 3):
        moved.append(along_tm(after(blocks[k - 1], d1, d2, d3), k))

    finals = []
    for i, arrays in enumerate(((first, c1, c2, c3), (second, d1, d2, d3))):
        keep, give = local_call(
            grad_kernel,
            [shape((group // 2, half), BF16)] * 2,
            [core_s],
            [heads, *arrays],
            [VMEM] + [HBM] * 4,
            [VMEM] * 2,
            scratch=[VMEM((4 * rows, half), BF16), VMEM((group, half), F32), dma((4,))],
            limit=8,
        )
        mine = add_rounded(keep, along_clip(give, 1))
        total = mine.astype(F32)
        for flip in (2, 4, 6):
            total = total + along_clip(mine, flip).astype(F32)
        mine = total.astype(BF16)
        finals += [mine, along_clip(after(mine, *moved[1:]) if i else mine, 1)]

    (encoded,) = local_call(
        project_kernel,
        [shape((rows, width), BF16)],
        [count_s],
        [hidden, *moved, w_all],
        [HBM] * 6,
        [HBM],
        scratch=[
            VMEM((rows, width), BF16),
            VMEM((rows, width), BF16),
            VMEM((width, width), BF16),
            VMEM((rows, width), BF16),
            dma((6,)),
        ],
        limit=10,
    )
    (grad_w_o,) = local_call(
        functools.partial(finish_kernel, 1.0 / math.sqrt(8 * rows * 4)),
        [shape((group, width), F32)],
        [after(core_s, encoded)],
        finals,
        [VMEM] * 4,
        [VMEM],
        limit=8,
    )
    return (encoded[None], grad_w_o)


def attend_call(me_s, packets, weights, rows, width):
    group = 4 * HEAD_DIM
    shape = jax.ShapeDtypeStruct
    scratch = [VMEM((4, *packets[0].shape), BF16)]
    scratch += [VMEM(w.shape, w.dtype) for w in weights]
    scratch += [VMEM((4 * rows, width), BF16)]
    scratch += [VMEM((4, 4 * rows, group), BF16)] * 3
    scratch += [pltpu.SemaphoreType.DMA((10,))]
    arrays = [*packets, *weights]
    return local_call(
        functools.partial(attend_kernel, rows),
        [
            shape((4 * rows, group), BF16),
            *[shape((rows, group), BF16)] * 3,
            shape((rows, width), BF16),
        ],
        [me_s],
        arrays,
        [HBM] * len(arrays),
        [VMEM] * 5,
        scratch=scratch,
        limit=63,
        cost=30000000,
    )


def solution(mesh):
    in_specs = (
        P("clip", "tm", None),
        P("clip", "tm"),
        P("clip", "tm"),
        P(),
        P(),
        P(),
        P(None, "tm"),
        P("tm", None),
        P("clip", "tm", None),
    )
    out_specs = (P("clip", "tm", None), P("tm", None))
    on_line = mesh.shape["tm"] == 4 and mesh.shape["clip"] == 8
    return jax.shard_map(
        line_device if on_line else general_device,
        mesh=mesh,
        in_specs=in_specs,
        out_specs=out_specs,
        check_vma=False,
    )
```

```python
import functools
import math

import jax
import jax.numpy as jnp
import ml_dtypes
import numpy as np
from jax import lax
from jax.experimental import pallas as pl
from jax.experimental.pallas import tpu as pltpu
from jax.sharding import PartitionSpec as P

HEAD_DIM = 64
PATCH_COLS = 80
PATCH_ROWS = 45
NEG_FILL = -1e30
NORM_EPS = 1e-05
F32 = jnp.float32
BF16 = jnp.bfloat16


def sincos_features(coord, width):
    half_width = width // 2
    step_ids = jnp.arange(half_width).astype(jnp.float32)
    frequency = 10000.0 ** (-step_ids / half_width)
    phase = coord.astype(jnp.float32)[:, None] * frequency[None, :]
    return jnp.concatenate([jnp.sin(phase), jnp.cos(phase)], axis=1)


def position_table(patch_ids, bin_ids, width):
    time_width = width // 4
    space_width = (width - time_width) // 2
    return jnp.concatenate(
        [
            sincos_features(bin_ids, time_width),
            sincos_features(patch_ids // PATCH_COLS, space_width),
            sincos_features(patch_ids % PATCH_COLS, space_width),
        ],
        axis=1,
    )


def layer_norm(rows_in, ln_gain):
    values = rows_in.astype(jnp.float32)
    row_mean = jnp.mean(values, axis=-1, keepdims=True)
    centred = values - row_mean
    variance = jnp.mean(centred * centred, axis=-1, keepdims=True)
    return (centred * lax.rsqrt(variance + NORM_EPS) * ln_gain.astype(jnp.float32)).astype(
        jnp.bfloat16
    )


def attend_heads(mixed_rows, key_valid):
    total_rows = mixed_rows.shape[0]
    heads_here = mixed_rows.shape[1] // (3 * HEAD_DIM)
    split_rows = mixed_rows.reshape(total_rows, heads_here, 3, HEAD_DIM)
    queries = split_rows[:, :, 0]
    keys_all = split_rows[:, :, 1]
    values_all = split_rows[:, :, 2]
    block_rows = math.gcd(total_rows, 512)
    query_blocks = queries.reshape(total_rows // block_rows, block_rows, heads_here, HEAD_DIM)
    score_scale = 1.0 / math.sqrt(HEAD_DIM)

    def one_block(query_block):
        scores = (
            jnp.einsum("qhd,khd->hqk", query_block, keys_all, preferred_element_type=jnp.float32)
            * score_scale
        )
        scores = jnp.where(key_valid[None, None, :], scores, NEG_FILL)
        row_max = jnp.max(scores, axis=2, keepdims=True)
        weights = jnp.exp(scores - row_max)
        weight_sum = jnp.sum(weights, axis=2, keepdims=True)
        mixed = jnp.einsum(
            "hqk,khd->qhd",
            weights.astype(jnp.bfloat16),
            values_all,
            preferred_element_type=jnp.float32,
        )
        return (mixed / weight_sum.transpose(1, 0, 2)).astype(jnp.bfloat16)

    outcome = lax.map(one_block, query_blocks)
    return outcome.reshape(total_rows, heads_here * HEAD_DIM)


def general_device(
    patches, patch_index, counts, w_embed, embed_bias, ln_gain, w_qkv, w_o, cotangent
):
    row_count = patches.shape[1]
    width = w_embed.shape[1]
    bin_total = lax.axis_size("tm")
    clip_total = lax.axis_size("clip")
    bin_now = lax.axis_index("tm")
    local_slots = jnp.arange(row_count)
    valid_rows = local_slots < counts[0, 0]
    bin_ids = jnp.zeros((row_count,), jnp.int32) + bin_now
    position = position_table(patch_index[0], bin_ids, width)
    embedded = jnp.dot(patches[0], w_embed, preferred_element_type=jnp.float32)
    embedded = embedded + embed_bias.astype(jnp.float32) + position
    hidden_rows = jnp.where(valid_rows[:, None], embedded, 0.0).astype(jnp.bfloat16)
    normed = layer_norm(hidden_rows, ln_gain)
    all_counts = lax.all_gather(counts, "tm", axis=1, tiled=True)
    key_slots = jnp.arange(row_count * bin_total)
    key_bins = key_slots // row_count
    bin_table = key_bins[:, None] == jnp.arange(bin_total)[None, :]
    key_count = jnp.sum(jnp.where(bin_table, all_counts[0][None, :], 0), axis=1)
    key_valid = key_slots % row_count < key_count
    mixed_rows = jnp.dot(
        lax.all_gather(normed, "tm", axis=0, tiled=True), w_qkv, preferred_element_type=jnp.float32
    ).astype(jnp.bfloat16)
    head_rows = attend_heads(mixed_rows, key_valid)
    attended = lax.all_to_all(head_rows, "tm", split_axis=0, concat_axis=1, tiled=True)
    projected = jnp.dot(
        attended, lax.all_gather(w_o, "tm", axis=0, tiled=True), preferred_element_type=jnp.float32
    )
    encoded = jnp.where(
        valid_rows[:, None], hidden_rows.astype(jnp.float32) + projected, 0.0
    ).astype(jnp.bfloat16)
    cot_rows = jnp.where(valid_rows[:, None], cotangent[0], jnp.zeros((), jnp.bfloat16))
    grad_scale = 1.0 / math.sqrt(clip_total * row_count * bin_total)
    grad_part = lax.psum_scatter(
        jnp.dot(attended.T, cot_rows, preferred_element_type=jnp.float32).astype(jnp.bfloat16),
        "tm",
        scatter_dimension=0,
        tiled=True,
    )
    grad_rows = lax.psum(grad_part, "clip").astype(jnp.float32)
    grad_w_o = grad_rows * grad_scale
    return (encoded[None], grad_w_o)


META = 16


def sincos_np(coord, width):
    half_width = width // 2
    frequency = 10000.0 ** (-np.arange(half_width) / half_width)
    phase = np.asarray(coord, np.float64)[:, None] * frequency[None, :]
    return np.concatenate([np.sin(phase), np.cos(phase)], axis=1)


def position_parts(bin_total, width):
    time_width = width // 4
    space_width = (width - time_width) // 2
    table = np.zeros((128, 2 * space_width), np.float64)
    table[:PATCH_ROWS, :space_width] = sincos_np(np.arange(PATCH_ROWS), space_width)
    table[PATCH_ROWS : PATCH_ROWS + PATCH_COLS, space_width:] = sincos_np(
        np.arange(PATCH_COLS), space_width
    )
    high = table.astype(ml_dtypes.bfloat16)
    low = (table - high.astype(np.float64)).astype(ml_dtypes.bfloat16)
    bins = np.zeros((8, time_width), np.float32)
    bins[:bin_total] = sincos_np(np.arange(bin_total), time_width)
    return np.concatenate([high, low], axis=0), bins


def local_call(kernel, out_shape, scalars, arrays, spaces, out_spaces, scratch=(), limit=16, cost=1000):
    specs = [pl.BlockSpec(memory_space=pltpu.SMEM)] * len(scalars)
    specs += [pl.BlockSpec(memory_space=space) for space in spaces]
    return pl.pallas_call(
        kernel,
        out_shape=out_shape,
        in_specs=specs,
        out_specs=[pl.BlockSpec(memory_space=space) for space in out_spaces],
        scratch_shapes=list(scratch),
        compiler_params=pltpu.CompilerParams(vmem_limit_bytes=limit * 1024 * 1024),
        cost_estimate=pl.CostEstimate(flops=1000, bytes_accessed=cost, transcendentals=0),
    )(*scalars, *arrays)


VMEM, HBM = pltpu.VMEM, pltpu.HBM


def pack_kernel(count_ref, patch_ref, index_ref, packet_ref, meta):
    rows = patch_ref.shape[0]
    packet_ref[0:rows, :] = patch_ref[...]
    numbers = jnp.clip(index_ref[...], 0, PATCH_ROWS * PATCH_COLS - 1).astype(F32)
    patch_row = jnp.floor((numbers + 0.5) * (1.0 / PATCH_COLS))
    meta[...] = jnp.full(meta.shape, 1.0, F32) * count_ref[0].astype(F32)
    meta[0:1, 0:rows] = patch_row
    meta[0:1, 256 : 256 + rows] = numbers - patch_row * PATCH_COLS
    packet_ref[rows:, :] = meta[...].astype(BF16)


def halve_kernel(clip_ref, cot_ref, w_ref, first_ref, second_ref):
    rows = cot_ref.shape[0]
    half = first_ref.shape[1]
    piece = w_ref.shape[0] // 8
    start = pl.multiple_of(clip_ref[0] * piece, piece)
    first_ref[0:rows, :] = cot_ref[:, 0:half]
    first_ref[rows : rows + piece, :] = w_ref[pl.ds(start, piece), 0:half]
    first_ref[rows + piece :, :] = w_ref[pl.ds(start, piece), half : 2 * half]
    second_ref[...] = cot_ref[:, half:]


def split_kernel(*refs):
    sources, piece_ref, sems = refs[:4], refs[4], refs[5]
    rows = sources[0].shape[0] - piece_ref.shape[1]
    copies = [
        pltpu.make_async_copy(source.at[rows:], piece_ref.at[k], sems.at[k])
        for k, source in enumerate(sources)
    ]
    for copy in copies:
        copy.start()
    for copy in copies:
        copy.wait()


def stage_kernel(w_qkv_ref, qkv_out):
    for part in range(3):
        for pair in range(2):
            first = (2 * pair * 3 + part) * HEAD_DIM
            second = first + 3 * HEAD_DIM
            both = jnp.concatenate(
                [
                    w_qkv_ref[:, first : first + HEAD_DIM],
                    w_qkv_ref[:, second : second + HEAD_DIM],
                ],
                axis=1,
            )
            at = (2 * part + pair) * 2 * HEAD_DIM
            qkv_out[:, at : at + 2 * HEAD_DIM] = both


def attend_kernel(
    rows,
    bin_ref,
    p0_hbm,
    p1_hbm,
    p2_hbm,
    p3_hbm,
    w_embed_hbm,
    table_hbm,
    bins_hbm,
    bias_hbm,
    gain_hbm,
    w_qkv_hbm,
    a_ref,
    a1_ref,
    a2_ref,
    a3_ref,
    hidden_ref,
    packets,
    w_embed_ref,
    table_ref,
    bins_ref,
    bias_ref,
    gain_ref,
    w_qkv_ref,
    normed_ref,
    q_ref,
    k_ref,
    v_ref,
    sems,
):
    me = bin_ref[0]
    copies = [
        pltpu.make_async_copy(source, packets.at[k], sems.at[k])
        for k, source in enumerate((p0_hbm, p1_hbm, p2_hbm, p3_hbm))
    ]
    for copy in copies:
        copy.start()
    staged = [
        pltpu.make_async_copy(source, target, sems.at[4 + i])
        for i, (source, target) in enumerate(
            (
                (w_embed_hbm, w_embed_ref),
                (table_hbm, table_ref),
                (bins_hbm, bins_ref),
                (bias_hbm, bias_ref),
                (gain_hbm, gain_ref),
                (w_qkv_hbm, w_qkv_ref),
            )
        )
    ]
    for copy in staged:
        copy.start()
    for copy in copies:
        copy.wait()
    for copy in staged[:-1]:
        copy.wait()
    group = 4 * HEAD_DIM
    slot = lax.broadcasted_iota(jnp.int32, (rows, 1), 0).astype(F32)
    place = lax.broadcasted_iota(jnp.int32, (128, rows), 0).astype(F32)
    lane = lax.broadcasted_iota(jnp.int32, (1, group), 1)
    bias = bias_ref[...].astype(F32)
    gain = gain_ref[...].astype(F32)
    owns, spares, spare_at = [], [], []
    for h in range(4):
        own = jnp.logical_and(lane >= h * HEAD_DIM, lane < (h + 1) * HEAD_DIM)
        spare_at.append((h * HEAD_DIM + group // 2) % group)
        owns.append(jnp.where(own, 1.0, 0.0).astype(BF16))
        spares.append(jnp.where(lane == spare_at[h], 1.0, 0.0))
    valid = []
    for k in range(4):
        here = slice(k * rows, (k + 1) * rows)
        meta = packets[k, rows:, :].astype(F32)
        ok = slot < meta[1:2, 0:1]
        valid.append(ok)
        hit = jnp.logical_or(
            place == meta[0:1, 0:rows], place == meta[0:1, 256 : 256 + rows] + PATCH_ROWS
        )
        hot = jnp.where(hit, 1.0, 0.0).astype(BF16)
        hot = jnp.concatenate([hot, hot], axis=0)
        space = lax.dot_general(
            hot, table_ref[...], (((0,), (0,)), ((), ())), preferred_element_type=F32
        )
        embedded = jnp.dot(packets[k, 0:rows, :], w_embed_ref[...], preferred_element_type=F32)
        times = bins_ref[pl.ds(jnp.bitwise_xor(me, k), 1), :]
        times = jnp.broadcast_to(times, (rows, times.shape[1]))
        embedded = embedded + bias + jnp.concatenate([times, space], axis=1)
        hidden = jnp.where(ok, embedded, 0.0).astype(BF16)
        if k == 0:
            hidden_ref[...] = hidden
        values = hidden.astype(F32)
        centred = values - jnp.mean(values, axis=1, keepdims=True)
        variance = jnp.mean(centred * centred, axis=1, keepdims=True)
        normed_ref[here, :] = (centred * lax.rsqrt(variance + NORM_EPS) * gain).astype(BF16)
    mask = jnp.concatenate([jnp.where(ok, 0.0, NEG_FILL) for ok in valid], axis=0)
    staged[-1].wait()
    for part, ref in enumerate((q_ref, k_ref, v_ref)):
        mixed = jnp.dot(
            normed_ref[...],
            w_qkv_ref[:, part * group : (part + 1) * group],
            preferred_element_type=F32,
        ).astype(BF16)
        if part == 0:
            mixed = mixed * jnp.asarray(1.0 / math.sqrt(HEAD_DIM), BF16)
        for h in range(4):
            fill = (mask * spares[h]).astype(BF16) if part == 1 else spares[h].astype(BF16)
            ref[h] = mixed * owns[h] + fill

    total = None
    for h in range(4):
        scores = lax.dot_general(
            q_ref[h], k_ref[h], (((1,), (1,)), ((), ())), preferred_element_type=F32
        )
        weights = jnp.exp(scores - jnp.max(scores, axis=1, keepdims=True)).astype(BF16)
        mixed = jnp.dot(weights, v_ref[h], preferred_element_type=F32)
        mixed = mixed * (1.0 / mixed[:, spare_at[h] : spare_at[h] + 1])
        total = mixed if h == 0 else jnp.where(owns[h] > 0, mixed, total)
    total = jnp.where(mask == 0.0, total, 0.0).astype(BF16)
    a_ref[...] = total
    for k, ref in enumerate((a1_ref, a2_ref, a3_ref)):
        ref[...] = total[(k + 1) * rows : (k + 2) * rows, :]


def grad_kernel(
    core_ref, a_ref, c0_hbm, c1_hbm, c2_hbm, c3_hbm, keep_ref, send_ref, cots, sum_ref, sems
):
    rows = cots.shape[0] // 4
    copies = [
        pltpu.make_async_copy(source.at[0:rows], cots.at[pl.ds(k * rows, rows)], sems.at[k])
        for k, source in enumerate((c0_hbm, c1_hbm, c2_hbm, c3_hbm))
    ]
    for copy in copies:
        copy.start()
    for copy in copies:
        copy.wait()
    sum_ref[...] = lax.dot_general(
        a_ref[...], cots[...], (((0,), (0,)), ((), ())), preferred_element_type=F32
    )
    half = sum_ref.shape[0] // 2
    core = core_ref[0]
    keep_ref[...] = sum_ref[pl.ds(pl.multiple_of(core * half, half), half), :].astype(BF16)
    send_ref[...] = sum_ref[pl.ds(pl.multiple_of((1 - core) * half, half), half), :].astype(BF16)


def project_kernel(clip_ref, count_ref, hidden_hbm, a0_hbm, a1_hbm, a2_hbm, a3_hbm, *refs):
    held, (out_hbm, hidden, heads, w_all, out, sems) = refs[:8], refs[8:]
    rows = hidden.shape[0]
    group = a0_hbm.shape[1]
    clip = clip_ref[0]
    piece = held[0].shape[1] // 2
    half = held[0].shape[2]
    copies = []

    def move(source, target):
        copies.append(pltpu.make_async_copy(source, target, sems.at[len(copies)]))
        copies[-1].start()

    for m in range(8):
        for k in range(4):
            start = pl.multiple_of(k * group + jnp.bitwise_xor(clip, m) * piece, piece)
            for side in range(2):
                move(
                    held[m].at[k, side * piece : (side + 1) * piece],
                    w_all.at[pl.ds(start, piece), side * half : (side + 1) * half],
                )
    move(hidden_hbm, hidden)
    move(a0_hbm.at[0:rows], heads.at[:, 0:group])
    for k, source in enumerate((a1_hbm, a2_hbm, a3_hbm)):
        move(source, heads.at[:, (k + 1) * group : (k + 2) * group])
    for copy in copies:
        copy.wait()
    slot = lax.broadcasted_iota(jnp.int32, (rows, 1), 0)
    projected = jnp.dot(heads[...], w_all[...], preferred_element_type=F32)
    total = hidden[...].astype(F32) + projected
    out[...] = jnp.where(slot < count_ref[0], total, 0.0).astype(BF16)
    write = pltpu.make_async_copy(out, out_hbm, sems.at[0])
    write.start()
    write.wait()


def finish_kernel(scale, core_ref, *refs):
    out_ref = refs[-1]
    core = core_ref[0]
    half = out_ref.shape[0] // 2
    mine = pl.multiple_of(core * half, half)
    theirs = pl.multiple_of((1 - core) * half, half)
    at = 0
    for c in range((len(refs) - 1) // 2):
        columns = slice(at, at + refs[2 * c].shape[1])
        at = columns.stop
        out_ref[pl.ds(mine, half), columns] = refs[2 * c][...].astype(F32) * scale
        out_ref[pl.ds(theirs, half), columns] = refs[2 * c + 1][...].astype(F32) * scale


def along_tm(array, flip):
    return lax.ppermute(array, "tm", [(i, i ^ flip) for i in range(4)])


def along_clip(array, flip):
    return lax.ppermute(array, "clip", [(i, i ^ flip) for i in range(8)])


def add_rounded(first, second):
    return (first.astype(F32) + second.astype(F32)).astype(BF16)


def after(value, *others):
    if not others:
        return value
    return lax.optimization_barrier((value, *others))[0]


def line_device(
    patches, patch_index, counts, w_embed, embed_bias, ln_gain, w_qkv, w_o, cotangent
):
    rows = patches.shape[1]
    half = patches.shape[2]
    width = w_embed.shape[1]
    group = 4 * HEAD_DIM
    piece = w_o.shape[0] // 8
    me = lax.axis_index("tm").astype(jnp.int32)
    clip = lax.axis_index("clip").astype(jnp.int32)
    core = clip % 2
    me_s, clip_s, core_s = me[None], clip[None], core[None]
    count_s = counts[0]
    shape = jax.ShapeDtypeStruct
    table, bins = position_parts(4, width)
    cot = cotangent[0]
    dma = pltpu.SemaphoreType.DMA

    extra = 2 * piece
    (packet,) = local_call(
        pack_kernel,
        [shape((rows + META, half), BF16)],
        [count_s],
        [patches[0], patch_index],
        [VMEM] * 2,
        [VMEM],
        scratch=[VMEM((META, half), F32)],
        limit=4,
    )
    first, second = local_call(
        halve_kernel,
        [
            shape((rows + extra, 512), BF16),
            shape((rows, width - 512), BF16),
        ],
        [clip_s],
        [cot, w_o],
        [VMEM] * 2,
        [VMEM] * 2,
        limit=4,
    )
    (w_ordered,) = local_call(
        stage_kernel, [shape((width, 3 * group), BF16)], [], [w_qkv], [VMEM], [VMEM], limit=8
    )
    bias_row, gain_row = embed_bias[None], ln_gain[None]
    p1, p2 = along_tm(packet, 1), along_tm(packet, 2)
    p3 = along_tm(after(packet), 3)
    c1 = along_tm(after(first, p1, w_ordered, bias_row, gain_row), 1)
    c2 = along_tm(after(first, p2), 2)
    c3 = along_tm(after(first, p1, p2, p3), 3)
    weights = [w_embed, jnp.asarray(table), jnp.asarray(bins), bias_row, gain_row]
    heads, *blocks, hidden = attend_call(
        me_s, [packet, p1, p2, after(p3)], [*weights, w_ordered], rows, width
    )
    d1 = along_tm(after(second, c1), 1)
    d2 = along_tm(after(second, heads), 2)
    d3 = along_tm(after(second, heads), 3)

    def reduce_clips(core, wide, arrays, two_rounds, *before):
        keep, give = local_call(
            grad_kernel,
            [shape((group // 2, wide), BF16)] * 2,
            [core],
            [heads, after(arrays[0], *before), *arrays[1:]],
            [VMEM] + [HBM] * 4,
            [VMEM] * 2,
            scratch=[VMEM((4 * rows, wide), BF16), VMEM((group, wide), F32), dma((4,))],
            limit=8,
        )
        mine = add_rounded(keep, along_clip(give, 1))
        if not two_rounds:
            total = mine.astype(F32)
            for flip in (2, 4, 6):
                total = total + along_clip(mine, flip).astype(F32)
            return total.astype(BF16)
        quarter = group // 4
        upper, lower = mine[:quarter], mine[quarter:]
        upper, lower = (
            add_rounded(upper, along_clip(upper, 2)),
            add_rounded(lower, along_clip(lower, 4)),
        )
        upper, lower = (
            add_rounded(upper, along_clip(upper, 4)),
            add_rounded(lower, along_clip(lower, 2)),
        )
        return jnp.concatenate([upper, lower], axis=0)

    sum_1 = reduce_clips(core_s, 512, (first, c1, c2, c3), False)

    (pieces,) = local_call(
        split_kernel,
        [shape((4, extra, half), BF16)],
        [],
        [first, c1, c2, c3],
        [HBM] * 4,
        [VMEM],
        scratch=[dma((4,))],
        limit=4,
    )
    pieces = after(pieces, d1)
    held = {0: pieces}
    held[2], held[4] = along_clip(pieces, 2), along_clip(pieces, 4)
    onward = jnp.where(core == 0, held[2], held[4])
    turn = [(i, i ^ 4) if i % 2 == 0 else (i, i ^ 2) for i in range(8)]
    held[6] = lax.ppermute(after(onward, heads), "clip", turn)
    for m in (0, 2, 4, 6):
        held[m + 1] = along_clip(held[m], 1)
    moved = [heads]
    for k in (1, 2, 3):
        moved.append(along_tm(after(blocks[k - 1], d2, d3), k))
    sum_2 = reduce_clips(core_s, width - 512, (second, d1, d2, d3), False)
    (encoded,) = local_call(
        project_kernel,
        [shape((rows, width), BF16)],
        [clip_s, count_s],
        [hidden, *moved, *[held[m] for m in range(8)]],
        [HBM] * 13,
        [HBM],
        scratch=[
            VMEM((rows, width), BF16),
            VMEM((rows, width), BF16),
            VMEM((width, width), BF16),
            VMEM((rows, width), BF16),
            dma((69,)),
        ],
        limit=10,
    )
    finals = [sum_1, along_clip(after(sum_1), 1)]
    finals += [sum_2, along_clip(after(sum_2, *moved[1:]), 1)]
    (grad_w_o,) = local_call(
        functools.partial(finish_kernel, 1.0 / math.sqrt(8 * rows * 4)),
        [shape((group, width), F32)],
        [after(core_s, encoded)],
        finals,
        [VMEM] * 4,
        [VMEM],
        limit=8,
    )
    return (encoded[None], grad_w_o)


def attend_call(me_s, packets, weights, rows, width):
    group = 4 * HEAD_DIM
    shape = jax.ShapeDtypeStruct
    scratch = [VMEM((4, *packets[0].shape), BF16)]
    scratch += [VMEM(w.shape, w.dtype) for w in weights]
    scratch += [VMEM((4 * rows, width), BF16)]
    scratch += [VMEM((4, 4 * rows, group), BF16)] * 3
    scratch += [pltpu.SemaphoreType.DMA((10,))]
    arrays = [*packets, *weights]
    return local_call(
        functools.partial(attend_kernel, rows),
        [
            shape((4 * rows, group), BF16),
            *[shape((rows, group), BF16)] * 3,
            shape((rows, width), BF16),
        ],
        [me_s],
        arrays,
        [HBM] * len(arrays),
        [VMEM] * 5,
        scratch=scratch,
        limit=63,
        cost=100000000,
    )


def solution(mesh):
    in_specs = (
        P("clip", "tm", None),
        P("clip", "tm"),
        P("clip", "tm"),
        P(),
        P(),
        P(),
        P(None, "tm"),
        P("tm", None),
        P("clip", "tm", None),
    )
    out_specs = (P("clip", "tm", None), P("tm", None))
    on_line = mesh.shape["tm"] == 4 and mesh.shape["clip"] == 8
    return jax.shard_map(
        line_device if on_line else general_device,
        mesh=mesh,
        in_specs=in_specs,
        out_specs=out_specs,
        check_vma=False,
    )
```

```python
import functools
import math

import jax
import jax.numpy as jnp
import ml_dtypes
import numpy as np
from jax import lax
from jax.experimental import pallas as pl
from jax.experimental.pallas import tpu as pltpu
from jax.sharding import PartitionSpec as P

HEAD_DIM = 64
PATCH_COLS = 80
PATCH_ROWS = 45
NEG_FILL = -1e30
NORM_EPS = 1e-05
F32 = jnp.float32
BF16 = jnp.bfloat16


def sincos_features(coord, width):
    half_width = width // 2
    step_ids = jnp.arange(half_width).astype(jnp.float32)
    frequency = 10000.0 ** (-step_ids / half_width)
    phase = coord.astype(jnp.float32)[:, None] * frequency[None, :]
    return jnp.concatenate([jnp.sin(phase), jnp.cos(phase)], axis=1)


def position_table(patch_ids, bin_ids, width):
    time_width = width // 4
    space_width = (width - time_width) // 2
    return jnp.concatenate(
        [
            sincos_features(bin_ids, time_width),
            sincos_features(patch_ids // PATCH_COLS, space_width),
            sincos_features(patch_ids % PATCH_COLS, space_width),
        ],
        axis=1,
    )


def layer_norm(rows_in, ln_gain):
    values = rows_in.astype(jnp.float32)
    row_mean = jnp.mean(values, axis=-1, keepdims=True)
    centred = values - row_mean
    variance = jnp.mean(centred * centred, axis=-1, keepdims=True)
    return (centred * lax.rsqrt(variance + NORM_EPS) * ln_gain.astype(jnp.float32)).astype(
        jnp.bfloat16
    )


def attend_heads(mixed_rows, key_valid):
    total_rows = mixed_rows.shape[0]
    heads_here = mixed_rows.shape[1] // (3 * HEAD_DIM)
    split_rows = mixed_rows.reshape(total_rows, heads_here, 3, HEAD_DIM)
    queries = split_rows[:, :, 0]
    keys_all = split_rows[:, :, 1]
    values_all = split_rows[:, :, 2]
    block_rows = math.gcd(total_rows, 512)
    query_blocks = queries.reshape(total_rows // block_rows, block_rows, heads_here, HEAD_DIM)
    score_scale = 1.0 / math.sqrt(HEAD_DIM)

    def one_block(query_block):
        scores = (
            jnp.einsum("qhd,khd->hqk", query_block, keys_all, preferred_element_type=jnp.float32)
            * score_scale
        )
        scores = jnp.where(key_valid[None, None, :], scores, NEG_FILL)
        row_max = jnp.max(scores, axis=2, keepdims=True)
        weights = jnp.exp(scores - row_max)
        weight_sum = jnp.sum(weights, axis=2, keepdims=True)
        mixed = jnp.einsum(
            "hqk,khd->qhd",
            weights.astype(jnp.bfloat16),
            values_all,
            preferred_element_type=jnp.float32,
        )
        return (mixed / weight_sum.transpose(1, 0, 2)).astype(jnp.bfloat16)

    outcome = lax.map(one_block, query_blocks)
    return outcome.reshape(total_rows, heads_here * HEAD_DIM)


def general_device(
    patches, patch_index, counts, w_embed, embed_bias, ln_gain, w_qkv, w_o, cotangent
):
    row_count = patches.shape[1]
    width = w_embed.shape[1]
    bin_total = lax.axis_size("tm")
    clip_total = lax.axis_size("clip")
    bin_now = lax.axis_index("tm")
    local_slots = jnp.arange(row_count)
    valid_rows = local_slots < counts[0, 0]
    bin_ids = jnp.zeros((row_count,), jnp.int32) + bin_now
    position = position_table(patch_index[0], bin_ids, width)
    embedded = jnp.dot(patches[0], w_embed, preferred_element_type=jnp.float32)
    embedded = embedded + embed_bias.astype(jnp.float32) + position
    hidden_rows = jnp.where(valid_rows[:, None], embedded, 0.0).astype(jnp.bfloat16)
    normed = layer_norm(hidden_rows, ln_gain)
    all_counts = lax.all_gather(counts, "tm", axis=1, tiled=True)
    key_slots = jnp.arange(row_count * bin_total)
    key_bins = key_slots // row_count
    bin_table = key_bins[:, None] == jnp.arange(bin_total)[None, :]
    key_count = jnp.sum(jnp.where(bin_table, all_counts[0][None, :], 0), axis=1)
    key_valid = key_slots % row_count < key_count
    mixed_rows = jnp.dot(
        lax.all_gather(normed, "tm", axis=0, tiled=True), w_qkv, preferred_element_type=jnp.float32
    ).astype(jnp.bfloat16)
    head_rows = attend_heads(mixed_rows, key_valid)
    attended = lax.all_to_all(head_rows, "tm", split_axis=0, concat_axis=1, tiled=True)
    projected = jnp.dot(
        attended, lax.all_gather(w_o, "tm", axis=0, tiled=True), preferred_element_type=jnp.float32
    )
    encoded = jnp.where(
        valid_rows[:, None], hidden_rows.astype(jnp.float32) + projected, 0.0
    ).astype(jnp.bfloat16)
    cot_rows = jnp.where(valid_rows[:, None], cotangent[0], jnp.zeros((), jnp.bfloat16))
    grad_scale = 1.0 / math.sqrt(clip_total * row_count * bin_total)
    grad_part = lax.psum_scatter(
        jnp.dot(attended.T, cot_rows, preferred_element_type=jnp.float32).astype(jnp.bfloat16),
        "tm",
        scatter_dimension=0,
        tiled=True,
    )
    grad_rows = lax.psum(grad_part, "clip").astype(jnp.float32)
    grad_w_o = grad_rows * grad_scale
    return (encoded[None], grad_w_o)


META = 16


def sincos_np(coord, width):
    half_width = width // 2
    frequency = 10000.0 ** (-np.arange(half_width) / half_width)
    phase = np.asarray(coord, np.float64)[:, None] * frequency[None, :]
    return np.concatenate([np.sin(phase), np.cos(phase)], axis=1)


def position_parts(bin_total, width):
    time_width = width // 4
    space_width = (width - time_width) // 2
    table = np.zeros((128, 2 * space_width), np.float64)
    table[:PATCH_ROWS, :space_width] = sincos_np(np.arange(PATCH_ROWS), space_width)
    table[PATCH_ROWS : PATCH_ROWS + PATCH_COLS, space_width:] = sincos_np(
        np.arange(PATCH_COLS), space_width
    )
    high = table.astype(ml_dtypes.bfloat16)
    low = (table - high.astype(np.float64)).astype(ml_dtypes.bfloat16)
    bins = np.zeros((8, time_width), np.float32)
    bins[:bin_total] = sincos_np(np.arange(bin_total), time_width)
    return np.concatenate([high, low], axis=0), bins


def local_call(kernel, out_shape, scalars, arrays, spaces, out_spaces, scratch=(), limit=16, cost=1000):
    specs = [pl.BlockSpec(memory_space=pltpu.SMEM)] * len(scalars)
    specs += [pl.BlockSpec(memory_space=space) for space in spaces]
    return pl.pallas_call(
        kernel,
        out_shape=out_shape,
        in_specs=specs,
        out_specs=[pl.BlockSpec(memory_space=space) for space in out_spaces],
        scratch_shapes=list(scratch),
        compiler_params=pltpu.CompilerParams(vmem_limit_bytes=limit * 1024 * 1024),
        cost_estimate=pl.CostEstimate(flops=1000, bytes_accessed=cost, transcendentals=0),
    )(*scalars, *arrays)


VMEM, HBM = pltpu.VMEM, pltpu.HBM


def pack_kernel(count_ref, patch_ref, index_ref, packet_ref, meta):
    rows = patch_ref.shape[0]
    packet_ref[0:rows, :] = patch_ref[...]
    numbers = jnp.clip(index_ref[...], 0, PATCH_ROWS * PATCH_COLS - 1).astype(F32)
    patch_row = jnp.floor((numbers + 0.5) * (1.0 / PATCH_COLS))
    meta[...] = jnp.full(meta.shape, 1.0, F32) * count_ref[0].astype(F32)
    meta[0:1, 0:rows] = patch_row
    meta[0:1, 256 : 256 + rows] = numbers - patch_row * PATCH_COLS
    packet_ref[rows:, :] = meta[...].astype(BF16)


def halve_kernel(clip_ref, cot_ref, w_ref, first_ref, second_ref):
    rows = cot_ref.shape[0]
    half = first_ref.shape[1]
    piece = w_ref.shape[0] // 8
    start = pl.multiple_of(clip_ref[0] * piece, piece)
    first_ref[0:rows, :] = cot_ref[:, 0:half]
    first_ref[rows : rows + piece, :] = w_ref[pl.ds(start, piece), 0:half]
    first_ref[rows + piece :, :] = w_ref[pl.ds(start, piece), half : 2 * half]
    second_ref[...] = cot_ref[:, half:]


def split_kernel(*refs):
    sources, piece_ref, sems = refs[:4], refs[4], refs[5]
    rows = sources[0].shape[0] - piece_ref.shape[1]
    copies = [
        pltpu.make_async_copy(source.at[rows:], piece_ref.at[k], sems.at[k])
        for k, source in enumerate(sources)
    ]
    for copy in copies:
        copy.start()
    for copy in copies:
        copy.wait()


def stage_kernel(w_qkv_ref, qkv_out):
    for part in range(3):
        for pair in range(2):
            first = (2 * pair * 3 + part) * HEAD_DIM
            second = first + 3 * HEAD_DIM
            both = jnp.concatenate(
                [
                    w_qkv_ref[:, first : first + HEAD_DIM],
                    w_qkv_ref[:, second : second + HEAD_DIM],
                ],
                axis=1,
            )
            at = (2 * part + pair) * 2 * HEAD_DIM
            qkv_out[:, at : at + 2 * HEAD_DIM] = both


def attend_kernel(
    rows,
    bin_ref,
    p0_hbm,
    p1_hbm,
    p2_hbm,
    p3_hbm,
    w_embed_hbm,
    table_hbm,
    bins_hbm,
    bias_hbm,
    gain_hbm,
    w_qkv_hbm,
    a_ref,
    a1_ref,
    a2_ref,
    a3_ref,
    hidden_ref,
    packets,
    w_embed_ref,
    table_ref,
    bins_ref,
    bias_ref,
    gain_ref,
    w_qkv_ref,
    normed_ref,
    q_ref,
    k_ref,
    v_ref,
    sems,
):
    me = bin_ref[0]
    copies = [
        pltpu.make_async_copy(source, packets.at[k], sems.at[k])
        for k, source in enumerate((p0_hbm, p1_hbm, p2_hbm, p3_hbm))
    ]
    for copy in copies:
        copy.start()
    staged = [
        pltpu.make_async_copy(source, target, sems.at[4 + i])
        for i, (source, target) in enumerate(
            (
                (w_embed_hbm, w_embed_ref),
                (table_hbm, table_ref),
                (bins_hbm, bins_ref),
                (bias_hbm, bias_ref),
                (gain_hbm, gain_ref),
                (w_qkv_hbm, w_qkv_ref),
            )
        )
    ]
    for copy in staged:
        copy.start()
    for copy in copies:
        copy.wait()
    for copy in staged[:-1]:
        copy.wait()
    group = 4 * HEAD_DIM
    slot = lax.broadcasted_iota(jnp.int32, (rows, 1), 0).astype(F32)
    place = lax.broadcasted_iota(jnp.int32, (128, rows), 0).astype(F32)
    lane = lax.broadcasted_iota(jnp.int32, (1, group), 1)
    bias = bias_ref[...].astype(F32)
    gain = gain_ref[...].astype(F32)
    owns, spares, spare_at = [], [], []
    for h in range(4):
        own = jnp.logical_and(lane >= h * HEAD_DIM, lane < (h + 1) * HEAD_DIM)
        spare_at.append((h * HEAD_DIM + group // 2) % group)
        owns.append(jnp.where(own, 1.0, 0.0).astype(BF16))
        spares.append(jnp.where(lane == spare_at[h], 1.0, 0.0))
    valid = []
    for k in range(4):
        here = slice(k * rows, (k + 1) * rows)
        meta = packets[k, rows:, :].astype(F32)
        ok = slot < meta[1:2, 0:1]
        valid.append(ok)
        hit = jnp.logical_or(
            place == meta[0:1, 0:rows], place == meta[0:1, 256 : 256 + rows] + PATCH_ROWS
        )
        hot = jnp.where(hit, 1.0, 0.0).astype(BF16)
        hot = jnp.concatenate([hot, hot], axis=0)
        space = lax.dot_general(
            hot, table_ref[...], (((0,), (0,)), ((), ())), preferred_element_type=F32
        )
        embedded = jnp.dot(packets[k, 0:rows, :], w_embed_ref[...], preferred_element_type=F32)
        times = bins_ref[pl.ds(jnp.bitwise_xor(me, k), 1), :]
        times = jnp.broadcast_to(times, (rows, times.shape[1]))
        embedded = embedded + bias + jnp.concatenate([times, space], axis=1)
        hidden = jnp.where(ok, embedded, 0.0).astype(BF16)
        if k == 0:
            hidden_ref[...] = hidden
        values = hidden.astype(F32)
        centred = values - jnp.mean(values, axis=1, keepdims=True)
        variance = jnp.mean(centred * centred, axis=1, keepdims=True)
        normed_ref[here, :] = (centred * lax.rsqrt(variance + NORM_EPS) * gain).astype(BF16)
    mask = jnp.concatenate([jnp.where(ok, 0.0, NEG_FILL) for ok in valid], axis=0)
    staged[-1].wait()
    for part, ref in enumerate((q_ref, k_ref, v_ref)):
        mixed = jnp.dot(
            normed_ref[...],
            w_qkv_ref[:, part * group : (part + 1) * group],
            preferred_element_type=F32,
        ).astype(BF16)
        if part == 0:
            mixed = mixed * jnp.asarray(1.0 / math.sqrt(HEAD_DIM), BF16)
        for h in range(4):
            fill = (mask * spares[h]).astype(BF16) if part == 1 else spares[h].astype(BF16)
            ref[h] = mixed * owns[h] + fill

    total = None
    for h in range(4):
        scores = lax.dot_general(
            q_ref[h], k_ref[h], (((1,), (1,)), ((), ())), preferred_element_type=F32
        )
        weights = jnp.exp(scores - jnp.max(scores, axis=1, keepdims=True)).astype(BF16)
        mixed = jnp.dot(weights, v_ref[h], preferred_element_type=F32)
        mixed = mixed * (1.0 / mixed[:, spare_at[h] : spare_at[h] + 1])
        total = mixed if h == 0 else jnp.where(owns[h] > 0, mixed, total)
    total = jnp.where(mask == 0.0, total, 0.0).astype(BF16)
    a_ref[...] = total
    for k, ref in enumerate((a1_ref, a2_ref, a3_ref)):
        ref[...] = total[(k + 1) * rows : (k + 2) * rows, :]


def grad_kernel(
    core_ref, a_ref, c0_hbm, c1_hbm, c2_hbm, c3_hbm, keep_ref, send_ref, cots, sum_ref, sems
):
    rows = cots.shape[0] // 4
    copies = [
        pltpu.make_async_copy(source.at[0:rows], cots.at[pl.ds(k * rows, rows)], sems.at[k])
        for k, source in enumerate((c0_hbm, c1_hbm, c2_hbm, c3_hbm))
    ]
    for copy in copies:
        copy.start()
    for copy in copies:
        copy.wait()
    sum_ref[...] = lax.dot_general(
        a_ref[...], cots[...], (((0,), (0,)), ((), ())), preferred_element_type=F32
    )
    half = sum_ref.shape[0] // 2
    core = core_ref[0]
    keep_ref[...] = sum_ref[pl.ds(pl.multiple_of(core * half, half), half), :].astype(BF16)
    send_ref[...] = sum_ref[pl.ds(pl.multiple_of((1 - core) * half, half), half), :].astype(BF16)


def project_kernel(clip_ref, count_ref, hidden_hbm, a0_hbm, a1_hbm, a2_hbm, a3_hbm, *refs):
    held, (out_hbm, hidden, heads, w_all, out, sems) = refs[:8], refs[8:]
    rows = hidden.shape[0]
    group = a0_hbm.shape[1]
    clip = clip_ref[0]
    piece = held[0].shape[1] // 2
    half = held[0].shape[2]
    copies = []

    def move(source, target):
        copies.append(pltpu.make_async_copy(source, target, sems.at[len(copies)]))
        copies[-1].start()

    for m in range(8):
        for k in range(4):
            start = pl.multiple_of(k * group + jnp.bitwise_xor(clip, m) * piece, piece)
            for side in range(2):
                move(
                    held[m].at[k, side * piece : (side + 1) * piece],
                    w_all.at[pl.ds(start, piece), side * half : (side + 1) * half],
                )
    move(hidden_hbm, hidden)
    move(a0_hbm.at[0:rows], heads.at[:, 0:group])
    for k, source in enumerate((a1_hbm, a2_hbm, a3_hbm)):
        move(source, heads.at[:, (k + 1) * group : (k + 2) * group])
    for copy in copies:
        copy.wait()
    slot = lax.broadcasted_iota(jnp.int32, (rows, 1), 0)
    projected = jnp.dot(heads[...], w_all[...], preferred_element_type=F32)
    total = hidden[...].astype(F32) + projected
    out[...] = jnp.where(slot < count_ref[0], total, 0.0).astype(BF16)
    write = pltpu.make_async_copy(out, out_hbm, sems.at[0])
    write.start()
    write.wait()


def finish_kernel(scale, core_ref, *refs):
    out_ref = refs[-1]
    core = core_ref[0]
    half = out_ref.shape[0] // 2
    mine = pl.multiple_of(core * half, half)
    theirs = pl.multiple_of((1 - core) * half, half)
    at = 0
    for c in range((len(refs) - 1) // 2):
        columns = slice(at, at + refs[2 * c].shape[1])
        at = columns.stop
        out_ref[pl.ds(mine, half), columns] = refs[2 * c][...].astype(F32) * scale
        out_ref[pl.ds(theirs, half), columns] = refs[2 * c + 1][...].astype(F32) * scale


def along_tm(array, flip):
    return lax.ppermute(array, "tm", [(i, i ^ flip) for i in range(4)])


def along_clip(array, flip):
    return lax.ppermute(array, "clip", [(i, i ^ flip) for i in range(8)])


def add_rounded(first, second):
    return (first.astype(F32) + second.astype(F32)).astype(BF16)


def after(value, *others):
    if not others:
        return value
    return lax.optimization_barrier((value, *others))[0]


def line_device(
    patches, patch_index, counts, w_embed, embed_bias, ln_gain, w_qkv, w_o, cotangent
):
    rows = patches.shape[1]
    half = patches.shape[2]
    width = w_embed.shape[1]
    group = 4 * HEAD_DIM
    piece = w_o.shape[0] // 8
    me = lax.axis_index("tm").astype(jnp.int32)
    clip = lax.axis_index("clip").astype(jnp.int32)
    core = clip % 2
    me_s, clip_s, core_s = me[None], clip[None], core[None]
    count_s = counts[0]
    shape = jax.ShapeDtypeStruct
    table, bins = position_parts(4, width)
    cot = cotangent[0]
    dma = pltpu.SemaphoreType.DMA

    extra = 2 * piece
    (packet,) = local_call(
        pack_kernel,
        [shape((rows + META, half), BF16)],
        [count_s],
        [patches[0], patch_index],
        [VMEM] * 2,
        [VMEM],
        scratch=[VMEM((META, half), F32)],
        limit=4,
    )
    first, second = local_call(
        halve_kernel,
        [
            shape((rows + extra, 512), BF16),
            shape((rows, width - 512), BF16),
        ],
        [clip_s],
        [cot, w_o],
        [VMEM] * 2,
        [VMEM] * 2,
        limit=4,
    )
    (w_ordered,) = local_call(
        stage_kernel, [shape((width, 3 * group), BF16)], [], [w_qkv], [VMEM], [VMEM], limit=8
    )
    bias_row, gain_row = embed_bias[None], ln_gain[None]
    p1, p2 = along_tm(packet, 1), along_tm(packet, 2)
    p3 = along_tm(after(packet), 3)
    c1 = along_tm(after(first, p1, w_ordered, bias_row, gain_row), 1)
    c2 = along_tm(after(first, p2), 2)
    c3 = along_tm(after(first, p1, p2, p3), 3)
    weights = [w_embed, jnp.asarray(table), jnp.asarray(bins), bias_row, gain_row]
    heads, *blocks, hidden = attend_call(
        me_s, [packet, p1, p2, after(p3)], [*weights, w_ordered], rows, width
    )
    d1 = along_tm(after(second, c1), 1)
    d2 = along_tm(after(second, heads), 2)
    d3 = along_tm(after(second, heads), 3)

    def reduce_clips(core, wide, arrays, two_rounds, *before):
        keep, give = local_call(
            grad_kernel,
            [shape((group // 2, wide), BF16)] * 2,
            [core],
            [heads, after(arrays[0], *before), *arrays[1:]],
            [VMEM] + [HBM] * 4,
            [VMEM] * 2,
            scratch=[VMEM((4 * rows, wide), BF16), VMEM((group, wide), F32), dma((4,))],
            limit=8,
        )
        mine = add_rounded(keep, along_clip(give, 1))
        if not two_rounds:
            total = mine.astype(F32)
            for flip in (2, 4, 6):
                total = total + along_clip(mine, flip).astype(F32)
            return total.astype(BF16)
        quarter = group // 4
        upper, lower = mine[:quarter], mine[quarter:]
        upper, lower = (
            add_rounded(upper, along_clip(upper, 2)),
            add_rounded(lower, along_clip(lower, 4)),
        )
        upper, lower = (
            add_rounded(upper, along_clip(upper, 4)),
            add_rounded(lower, along_clip(lower, 2)),
        )
        return jnp.concatenate([upper, lower], axis=0)

    sum_1 = reduce_clips(core_s, 512, (first, c1, c2, c3), False)

    (pieces,) = local_call(
        split_kernel,
        [shape((4, extra, half), BF16)],
        [],
        [first, c1, c2, c3],
        [HBM] * 4,
        [VMEM],
        scratch=[dma((4,))],
        limit=4,
    )
    pieces = after(pieces, d1, d2)
    held = {0: pieces}
    held[2], held[4] = along_clip(pieces, 2), along_clip(pieces, 4)
    onward = jnp.where(core == 0, held[2], held[4])
    turn = [(i, i ^ 4) if i % 2 == 0 else (i, i ^ 2) for i in range(8)]
    held[6] = lax.ppermute(after(onward, heads), "clip", turn)
    for m in (0, 2, 4, 6):
        held[m + 1] = along_clip(held[m], 1)
    moved = [heads]
    for k in (1, 2, 3):
        moved.append(along_tm(after(blocks[k - 1], d2, d3), k))
    sum_2 = reduce_clips(core_s, width - 512, (second, d1, d2, d3), False)
    (encoded,) = local_call(
        project_kernel,
        [shape((rows, width), BF16)],
        [clip_s, count_s],
        [hidden, *moved, *[held[m] for m in range(8)]],
        [HBM] * 13,
        [HBM],
        scratch=[
            VMEM((rows, width), BF16),
            VMEM((rows, width), BF16),
            VMEM((width, width), BF16),
            VMEM((rows, width), BF16),
            dma((69,)),
        ],
        limit=10,
    )
    finals = [sum_1, along_clip(after(sum_1), 1)]
    finals += [sum_2, along_clip(after(sum_2, *moved[1:]), 1)]
    (grad_w_o,) = local_call(
        functools.partial(finish_kernel, 1.0 / math.sqrt(8 * rows * 4)),
        [shape((group, width), F32)],
        [after(core_s, encoded)],
        finals,
        [VMEM] * 4,
        [VMEM],
        limit=8,
    )
    return (encoded[None], grad_w_o)


def attend_call(me_s, packets, weights, rows, width):
    group = 4 * HEAD_DIM
    shape = jax.ShapeDtypeStruct
    scratch = [VMEM((4, *packets[0].shape), BF16)]
    scratch += [VMEM(w.shape, w.dtype) for w in weights]
    scratch += [VMEM((4 * rows, width), BF16)]
    scratch += [VMEM((4, 4 * rows, group), BF16)] * 3
    scratch += [pltpu.SemaphoreType.DMA((10,))]
    arrays = [*packets, *weights]
    return local_call(
        functools.partial(attend_kernel, rows),
        [
            shape((4 * rows, group), BF16),
            *[shape((rows, group), BF16)] * 3,
            shape((rows, width), BF16),
        ],
        [me_s],
        arrays,
        [HBM] * len(arrays),
        [VMEM] * 5,
        scratch=scratch,
        limit=63,
        cost=100000000,
    )


def solution(mesh):
    in_specs = (
        P("clip", "tm", None),
        P("clip", "tm"),
        P("clip", "tm"),
        P(),
        P(),
        P(),
        P(None, "tm"),
        P("tm", None),
        P("clip", "tm", None),
    )
    out_specs = (P("clip", "tm", None), P("tm", None))
    on_line = mesh.shape["tm"] == 4 and mesh.shape["clip"] == 8
    return jax.shard_map(
        line_device if on_line else general_device,
        mesh=mesh,
        in_specs=in_specs,
        out_specs=out_specs,
        check_vma=False,
    )
```

```python
import functools
import math

import jax
import jax.numpy as jnp
import ml_dtypes
import numpy as np
from jax import lax
from jax.experimental import pallas as pl
from jax.experimental.pallas import tpu as pltpu
from jax.sharding import PartitionSpec as P

HEAD_DIM = 64
PATCH_COLS = 80
PATCH_ROWS = 45
NEG_FILL = -1e30
NORM_EPS = 1e-05
F32 = jnp.float32
BF16 = jnp.bfloat16


def sincos_features(coord, width):
    half_width = width // 2
    step_ids = jnp.arange(half_width).astype(jnp.float32)
    frequency = 10000.0 ** (-step_ids / half_width)
    phase = coord.astype(jnp.float32)[:, None] * frequency[None, :]
    return jnp.concatenate([jnp.sin(phase), jnp.cos(phase)], axis=1)


def position_table(patch_ids, bin_ids, width):
    time_width = width // 4
    space_width = (width - time_width) // 2
    return jnp.concatenate(
        [
            sincos_features(bin_ids, time_width),
            sincos_features(patch_ids // PATCH_COLS, space_width),
            sincos_features(patch_ids % PATCH_COLS, space_width),
        ],
        axis=1,
    )


def layer_norm(rows_in, ln_gain):
    values = rows_in.astype(jnp.float32)
    row_mean = jnp.mean(values, axis=-1, keepdims=True)
    centred = values - row_mean
    variance = jnp.mean(centred * centred, axis=-1, keepdims=True)
    return (centred * lax.rsqrt(variance + NORM_EPS) * ln_gain.astype(jnp.float32)).astype(
        jnp.bfloat16
    )


def attend_heads(mixed_rows, key_valid):
    total_rows = mixed_rows.shape[0]
    heads_here = mixed_rows.shape[1] // (3 * HEAD_DIM)
    split_rows = mixed_rows.reshape(total_rows, heads_here, 3, HEAD_DIM)
    queries = split_rows[:, :, 0]
    keys_all = split_rows[:, :, 1]
    values_all = split_rows[:, :, 2]
    block_rows = math.gcd(total_rows, 512)
    query_blocks = queries.reshape(total_rows // block_rows, block_rows, heads_here, HEAD_DIM)
    score_scale = 1.0 / math.sqrt(HEAD_DIM)

    def one_block(query_block):
        scores = (
            jnp.einsum("qhd,khd->hqk", query_block, keys_all, preferred_element_type=jnp.float32)
            * score_scale
        )
        scores = jnp.where(key_valid[None, None, :], scores, NEG_FILL)
        row_max = jnp.max(scores, axis=2, keepdims=True)
        weights = jnp.exp(scores - row_max)
        weight_sum = jnp.sum(weights, axis=2, keepdims=True)
        mixed = jnp.einsum(
            "hqk,khd->qhd",
            weights.astype(jnp.bfloat16),
            values_all,
            preferred_element_type=jnp.float32,
        )
        return (mixed / weight_sum.transpose(1, 0, 2)).astype(jnp.bfloat16)

    outcome = lax.map(one_block, query_blocks)
    return outcome.reshape(total_rows, heads_here * HEAD_DIM)


def general_device(
    patches, patch_index, counts, w_embed, embed_bias, ln_gain, w_qkv, w_o, cotangent
):
    row_count = patches.shape[1]
    width = w_embed.shape[1]
    bin_total = lax.axis_size("tm")
    clip_total = lax.axis_size("clip")
    bin_now = lax.axis_index("tm")
    local_slots = jnp.arange(row_count)
    valid_rows = local_slots < counts[0, 0]
    bin_ids = jnp.zeros((row_count,), jnp.int32) + bin_now
    position = position_table(patch_index[0], bin_ids, width)
    embedded = jnp.dot(patches[0], w_embed, preferred_element_type=jnp.float32)
    embedded = embedded + embed_bias.astype(jnp.float32) + position
    hidden_rows = jnp.where(valid_rows[:, None], embedded, 0.0).astype(jnp.bfloat16)
    normed = layer_norm(hidden_rows, ln_gain)
    all_counts = lax.all_gather(counts, "tm", axis=1, tiled=True)
    key_slots = jnp.arange(row_count * bin_total)
    key_bins = key_slots // row_count
    bin_table = key_bins[:, None] == jnp.arange(bin_total)[None, :]
    key_count = jnp.sum(jnp.where(bin_table, all_counts[0][None, :], 0), axis=1)
    key_valid = key_slots % row_count < key_count
    mixed_rows = jnp.dot(
        lax.all_gather(normed, "tm", axis=0, tiled=True), w_qkv, preferred_element_type=jnp.float32
    ).astype(jnp.bfloat16)
    head_rows = attend_heads(mixed_rows, key_valid)
    attended = lax.all_to_all(head_rows, "tm", split_axis=0, concat_axis=1, tiled=True)
    projected = jnp.dot(
        attended, lax.all_gather(w_o, "tm", axis=0, tiled=True), preferred_element_type=jnp.float32
    )
    encoded = jnp.where(
        valid_rows[:, None], hidden_rows.astype(jnp.float32) + projected, 0.0
    ).astype(jnp.bfloat16)
    cot_rows = jnp.where(valid_rows[:, None], cotangent[0], jnp.zeros((), jnp.bfloat16))
    grad_scale = 1.0 / math.sqrt(clip_total * row_count * bin_total)
    grad_part = lax.psum_scatter(
        jnp.dot(attended.T, cot_rows, preferred_element_type=jnp.float32).astype(jnp.bfloat16),
        "tm",
        scatter_dimension=0,
        tiled=True,
    )
    grad_rows = lax.psum(grad_part, "clip").astype(jnp.float32)
    grad_w_o = grad_rows * grad_scale
    return (encoded[None], grad_w_o)


META = 16


def sincos_np(coord, width):
    half_width = width // 2
    frequency = 10000.0 ** (-np.arange(half_width) / half_width)
    phase = np.asarray(coord, np.float64)[:, None] * frequency[None, :]
    return np.concatenate([np.sin(phase), np.cos(phase)], axis=1)


def position_parts(bin_total, width):
    time_width = width // 4
    space_width = (width - time_width) // 2
    table = np.zeros((128, 2 * space_width), np.float64)
    table[:PATCH_ROWS, :space_width] = sincos_np(np.arange(PATCH_ROWS), space_width)
    table[PATCH_ROWS : PATCH_ROWS + PATCH_COLS, space_width:] = sincos_np(
        np.arange(PATCH_COLS), space_width
    )
    high = table.astype(ml_dtypes.bfloat16)
    low = (table - high.astype(np.float64)).astype(ml_dtypes.bfloat16)
    bins = np.zeros((8, time_width), np.float32)
    bins[:bin_total] = sincos_np(np.arange(bin_total), time_width)
    return np.concatenate([high, low], axis=0), bins


def local_call(kernel, out_shape, scalars, arrays, spaces, out_spaces, scratch=(), limit=16, cost=1000):
    specs = [pl.BlockSpec(memory_space=pltpu.SMEM)] * len(scalars)
    specs += [pl.BlockSpec(memory_space=space) for space in spaces]
    return pl.pallas_call(
        kernel,
        out_shape=out_shape,
        in_specs=specs,
        out_specs=[pl.BlockSpec(memory_space=space) for space in out_spaces],
        scratch_shapes=list(scratch),
        compiler_params=pltpu.CompilerParams(vmem_limit_bytes=limit * 1024 * 1024),
        cost_estimate=pl.CostEstimate(flops=1000, bytes_accessed=cost, transcendentals=0),
    )(*scalars, *arrays)


VMEM, HBM = pltpu.VMEM, pltpu.HBM


def pack_kernel(count_ref, patch_ref, index_ref, packet_ref, meta):
    rows = patch_ref.shape[0]
    packet_ref[0:rows, :] = patch_ref[...]
    numbers = jnp.clip(index_ref[...], 0, PATCH_ROWS * PATCH_COLS - 1).astype(F32)
    patch_row = jnp.floor((numbers + 0.5) * (1.0 / PATCH_COLS))
    meta[...] = jnp.full(meta.shape, 1.0, F32) * count_ref[0].astype(F32)
    meta[0:1, 0:rows] = patch_row
    meta[0:1, 256 : 256 + rows] = numbers - patch_row * PATCH_COLS
    packet_ref[rows:, :] = meta[...].astype(BF16)


def halve_kernel(clip_ref, cot_ref, w_ref, first_ref, second_ref):
    rows = cot_ref.shape[0]
    half = first_ref.shape[1]
    piece = w_ref.shape[0] // 8
    start = pl.multiple_of(clip_ref[0] * piece, piece)
    first_ref[0:rows, :] = cot_ref[:, 0:half]
    first_ref[rows : rows + piece, :] = w_ref[pl.ds(start, piece), 0:half]
    first_ref[rows + piece :, :] = w_ref[pl.ds(start, piece), half : 2 * half]
    second_ref[...] = cot_ref[:, half:]


def split_kernel(*refs):
    sources, piece_ref, sems = refs[:4], refs[4], refs[5]
    rows = sources[0].shape[0] - piece_ref.shape[1]
    copies = [
        pltpu.make_async_copy(source.at[rows:], piece_ref.at[k], sems.at[k])
        for k, source in enumerate(sources)
    ]
    for copy in copies:
        copy.start()
    for copy in copies:
        copy.wait()


def stage_kernel(w_qkv_ref, qkv_out):
    for part in range(3):
        for pair in range(2):
            first = (2 * pair * 3 + part) * HEAD_DIM
            second = first + 3 * HEAD_DIM
            both = jnp.concatenate(
                [
                    w_qkv_ref[:, first : first + HEAD_DIM],
                    w_qkv_ref[:, second : second + HEAD_DIM],
                ],
                axis=1,
            )
            at = (2 * part + pair) * 2 * HEAD_DIM
            qkv_out[:, at : at + 2 * HEAD_DIM] = both


def attend_kernel(
    rows,
    bin_ref,
    p0_hbm,
    p1_hbm,
    p2_hbm,
    p3_hbm,
    w_embed_hbm,
    table_hbm,
    bins_hbm,
    bias_hbm,
    gain_hbm,
    w_qkv_hbm,
    a_ref,
    a1_ref,
    a2_ref,
    a3_ref,
    hidden_ref,
    packets,
    w_embed_ref,
    table_ref,
    bins_ref,
    bias_ref,
    gain_ref,
    w_qkv_ref,
    normed_ref,
    q_ref,
    k_ref,
    v_ref,
    sems,
):
    me = bin_ref[0]
    copies = [
        pltpu.make_async_copy(source, packets.at[k], sems.at[k])
        for k, source in enumerate((p0_hbm, p1_hbm, p2_hbm, p3_hbm))
    ]
    for copy in copies:
        copy.start()
    staged = [
        pltpu.make_async_copy(source, target, sems.at[4 + i])
        for i, (source, target) in enumerate(
            (
                (w_embed_hbm, w_embed_ref),
                (table_hbm, table_ref),
                (bins_hbm, bins_ref),
                (bias_hbm, bias_ref),
                (gain_hbm, gain_ref),
                (w_qkv_hbm, w_qkv_ref),
            )
        )
    ]
    for copy in staged:
        copy.start()
    for copy in copies:
        copy.wait()
    for copy in staged[:-1]:
        copy.wait()
    group = 4 * HEAD_DIM
    slot = lax.broadcasted_iota(jnp.int32, (rows, 1), 0).astype(F32)
    place = lax.broadcasted_iota(jnp.int32, (128, rows), 0).astype(F32)
    lane = lax.broadcasted_iota(jnp.int32, (1, group), 1)
    bias = bias_ref[...].astype(F32)
    gain = gain_ref[...].astype(F32)
    owns, spares, spare_at = [], [], []
    for h in range(4):
        own = jnp.logical_and(lane >= h * HEAD_DIM, lane < (h + 1) * HEAD_DIM)
        spare_at.append((h * HEAD_DIM + group // 2) % group)
        owns.append(jnp.where(own, 1.0, 0.0).astype(BF16))
        spares.append(jnp.where(lane == spare_at[h], 1.0, 0.0))
    valid = []
    for k in range(4):
        here = slice(k * rows, (k + 1) * rows)
        meta = packets[k, rows:, :].astype(F32)
        ok = slot < meta[1:2, 0:1]
        valid.append(ok)
        hit = jnp.logical_or(
            place == meta[0:1, 0:rows], place == meta[0:1, 256 : 256 + rows] + PATCH_ROWS
        )
        hot = jnp.where(hit, 1.0, 0.0).astype(BF16)
        hot = jnp.concatenate([hot, hot], axis=0)
        space = lax.dot_general(
            hot, table_ref[...], (((0,), (0,)), ((), ())), preferred_element_type=F32
        )
        embedded = jnp.dot(packets[k, 0:rows, :], w_embed_ref[...], preferred_element_type=F32)
        times = bins_ref[pl.ds(jnp.bitwise_xor(me, k), 1), :]
        times = jnp.broadcast_to(times, (rows, times.shape[1]))
        embedded = embedded + bias + jnp.concatenate([times, space], axis=1)
        hidden = jnp.where(ok, embedded, 0.0).astype(BF16)
        if k == 0:
            hidden_ref[...] = hidden
        values = hidden.astype(F32)
        centred = values - jnp.mean(values, axis=1, keepdims=True)
        variance = jnp.mean(centred * centred, axis=1, keepdims=True)
        normed_ref[here, :] = (centred * lax.rsqrt(variance + NORM_EPS) * gain).astype(BF16)
    mask = jnp.concatenate([jnp.where(ok, 0.0, NEG_FILL) for ok in valid], axis=0)
    staged[-1].wait()
    for part, ref in enumerate((q_ref, k_ref, v_ref)):
        mixed = jnp.dot(
            normed_ref[...],
            w_qkv_ref[:, part * group : (part + 1) * group],
            preferred_element_type=F32,
        ).astype(BF16)
        if part == 0:
            mixed = mixed * jnp.asarray(1.0 / math.sqrt(HEAD_DIM), BF16)
        for h in range(4):
            fill = (mask * spares[h]).astype(BF16) if part == 1 else spares[h].astype(BF16)
            ref[h] = mixed * owns[h] + fill

    total = None
    for h in range(4):
        scores = lax.dot_general(
            q_ref[h], k_ref[h], (((1,), (1,)), ((), ())), preferred_element_type=F32
        )
        weights = jnp.exp(scores - jnp.max(scores, axis=1, keepdims=True)).astype(BF16)
        mixed = jnp.dot(weights, v_ref[h], preferred_element_type=F32)
        mixed = mixed * (1.0 / mixed[:, spare_at[h] : spare_at[h] + 1])
        total = mixed if h == 0 else jnp.where(owns[h] > 0, mixed, total)
    total = jnp.where(mask == 0.0, total, 0.0).astype(BF16)
    a_ref[...] = total
    for k, ref in enumerate((a1_ref, a2_ref, a3_ref)):
        ref[...] = total[(k + 1) * rows : (k + 2) * rows, :]


def grad_kernel(
    core_ref, a_ref, c0_hbm, c1_hbm, c2_hbm, c3_hbm, keep_ref, send_ref, cots, sum_ref, sems
):
    rows = cots.shape[0] // 4
    copies = [
        pltpu.make_async_copy(source.at[0:rows], cots.at[pl.ds(k * rows, rows)], sems.at[k])
        for k, source in enumerate((c0_hbm, c1_hbm, c2_hbm, c3_hbm))
    ]
    for copy in copies:
        copy.start()
    for copy in copies:
        copy.wait()
    sum_ref[...] = lax.dot_general(
        a_ref[...], cots[...], (((0,), (0,)), ((), ())), preferred_element_type=F32
    )
    half = sum_ref.shape[0] // 2
    core = core_ref[0]
    keep_ref[...] = sum_ref[pl.ds(pl.multiple_of(core * half, half), half), :].astype(BF16)
    send_ref[...] = sum_ref[pl.ds(pl.multiple_of((1 - core) * half, half), half), :].astype(BF16)


def project_kernel(clip_ref, count_ref, hidden_hbm, a0_hbm, a1_hbm, a2_hbm, a3_hbm, *refs):
    held, (out_hbm, hidden, heads, w_all, out, sems) = refs[:8], refs[8:]
    rows = hidden.shape[0]
    group = a0_hbm.shape[1]
    clip = clip_ref[0]
    piece = held[0].shape[1] // 2
    half = held[0].shape[2]
    copies = []

    def move(source, target):
        copies.append(pltpu.make_async_copy(source, target, sems.at[len(copies)]))
        copies[-1].start()

    for m in range(8):
        move(held[m], w_all.at[:, jnp.bitwise_xor(clip, m)])
    move(hidden_hbm, hidden)
    move(a0_hbm.at[0:rows], heads.at[:, 0:group])
    for k, source in enumerate((a1_hbm, a2_hbm, a3_hbm)):
        move(source, heads.at[:, (k + 1) * group : (k + 2) * group])
    for copy in copies:
        copy.wait()
    slot = lax.broadcasted_iota(jnp.int32, (rows, 1), 0)
    depth = 32 * piece
    sides = [
        jnp.dot(
            heads[...],
            w_all[:, :, side * piece : (side + 1) * piece, :].reshape(depth, half),
            preferred_element_type=F32,
        )
        for side in range(2)
    ]
    projected = jnp.concatenate(sides, axis=1)
    total = hidden[...].astype(F32) + projected
    out[...] = jnp.where(slot < count_ref[0], total, 0.0).astype(BF16)
    write = pltpu.make_async_copy(out, out_hbm, sems.at[0])
    write.start()
    write.wait()


def finish_kernel(scale, core_ref, *refs):
    out_ref = refs[-1]
    core = core_ref[0]
    half = out_ref.shape[0] // 2
    mine = pl.multiple_of(core * half, half)
    theirs = pl.multiple_of((1 - core) * half, half)
    at = 0
    for c in range((len(refs) - 1) // 2):
        columns = slice(at, at + refs[2 * c].shape[1])
        at = columns.stop
        out_ref[pl.ds(mine, half), columns] = refs[2 * c][...].astype(F32) * scale
        out_ref[pl.ds(theirs, half), columns] = refs[2 * c + 1][...].astype(F32) * scale


def along_tm(array, flip):
    return lax.ppermute(array, "tm", [(i, i ^ flip) for i in range(4)])


def along_clip(array, flip):
    return lax.ppermute(array, "clip", [(i, i ^ flip) for i in range(8)])


def add_rounded(first, second):
    return (first.astype(F32) + second.astype(F32)).astype(BF16)


def after(value, *others):
    if not others:
        return value
    return lax.optimization_barrier((value, *others))[0]


def line_device(
    patches, patch_index, counts, w_embed, embed_bias, ln_gain, w_qkv, w_o, cotangent
):
    rows = patches.shape[1]
    half = patches.shape[2]
    width = w_embed.shape[1]
    group = 4 * HEAD_DIM
    piece = w_o.shape[0] // 8
    me = lax.axis_index("tm").astype(jnp.int32)
    clip = lax.axis_index("clip").astype(jnp.int32)
    core = clip % 2
    me_s, clip_s, core_s = me[None], clip[None], core[None]
    count_s = counts[0]
    shape = jax.ShapeDtypeStruct
    table, bins = position_parts(4, width)
    cot = cotangent[0]
    dma = pltpu.SemaphoreType.DMA

    extra = 2 * piece
    (packet,) = local_call(
        pack_kernel,
        [shape((rows + META, half), BF16)],
        [count_s],
        [patches[0], patch_index],
        [VMEM] * 2,
        [VMEM],
        scratch=[VMEM((META, half), F32)],
        limit=4,
    )
    first, second = local_call(
        halve_kernel,
        [
            shape((rows + extra, 512), BF16),
            shape((rows, width - 512), BF16),
        ],
        [clip_s],
        [cot, w_o],
        [VMEM] * 2,
        [VMEM] * 2,
        limit=4,
    )
    (w_ordered,) = local_call(
        stage_kernel, [shape((width, 3 * group), BF16)], [], [w_qkv], [VMEM], [VMEM], limit=8
    )
    bias_row, gain_row = embed_bias[None], ln_gain[None]
    p1, p2 = along_tm(packet, 1), along_tm(packet, 2)
    p3 = along_tm(after(packet), 3)
    c1 = along_tm(after(first, p1, w_ordered, bias_row, gain_row), 1)
    c2 = along_tm(after(first, p2), 2)
    c3 = along_tm(after(first, p1, p2, p3), 3)
    weights = [w_embed, jnp.asarray(table), jnp.asarray(bins), bias_row, gain_row]
    heads, *blocks, hidden = attend_call(
        me_s, [packet, p1, p2, after(p3)], [*weights, w_ordered], rows, width
    )
    d1 = along_tm(after(second, c1), 1)
    d2 = along_tm(after(second, heads), 2)
    d3 = along_tm(after(second, heads), 3)

    def reduce_clips(core, wide, arrays, two_rounds, *before):
        keep, give = local_call(
            grad_kernel,
            [shape((group // 2, wide), BF16)] * 2,
            [core],
            [heads, after(arrays[0], *before), *arrays[1:]],
            [VMEM] + [HBM] * 4,
            [VMEM] * 2,
            scratch=[VMEM((4 * rows, wide), BF16), VMEM((group, wide), F32), dma((4,))],
            limit=8,
        )
        mine = add_rounded(keep, along_clip(give, 1))
        if not two_rounds:
            total = mine.astype(F32)
            for flip in (2, 4, 6):
                total = total + along_clip(mine, flip).astype(F32)
            return total.astype(BF16)
        quarter = group // 4
        upper, lower = mine[:quarter], mine[quarter:]
        upper, lower = (
            add_rounded(upper, along_clip(upper, 2)),
            add_rounded(lower, along_clip(lower, 4)),
        )
        upper, lower = (
            add_rounded(upper, along_clip(upper, 4)),
            add_rounded(lower, along_clip(lower, 2)),
        )
        return jnp.concatenate([upper, lower], axis=0)

    sum_1 = reduce_clips(core_s, 512, (first, c1, c2, c3), False)

    (pieces,) = local_call(
        split_kernel,
        [shape((4, extra, half), BF16)],
        [],
        [first, c1, c2, c3],
        [HBM] * 4,
        [VMEM],
        scratch=[dma((4,))],
        limit=4,
    )
    pieces = after(pieces, d1, d2)
    held = {0: pieces}
    held[2], held[4] = along_clip(pieces, 2), along_clip(pieces, 4)
    onward = jnp.where(core == 0, held[2], held[4])
    turn = [(i, i ^ 4) if i % 2 == 0 else (i, i ^ 2) for i in range(8)]
    held[6] = lax.ppermute(after(onward, heads), "clip", turn)
    for m in (0, 2, 4, 6):
        held[m + 1] = along_clip(held[m], 1)
    moved = [heads]
    for k in (1, 2, 3):
        moved.append(along_tm(after(blocks[k - 1], d2, d3), k))
    sum_2 = reduce_clips(core_s, width - 512, (second, d1, d2, d3), False)
    (encoded,) = local_call(
        project_kernel,
        [shape((rows, width), BF16)],
        [clip_s, count_s],
        [hidden, *moved, *[held[m] for m in range(8)]],
        [HBM] * 13,
        [HBM],
        scratch=[
            VMEM((rows, width), BF16),
            VMEM((rows, width), BF16),
            VMEM((4, 8, extra, half), BF16),
            VMEM((rows, width), BF16),
            dma((13,)),
        ],
        limit=10,
    )
    finals = [sum_1, along_clip(after(sum_1), 1)]
    finals += [sum_2, along_clip(after(sum_2, *moved[1:]), 1)]
    (grad_w_o,) = local_call(
        functools.partial(finish_kernel, 1.0 / math.sqrt(8 * rows * 4)),
        [shape((group, width), F32)],
        [after(core_s, encoded)],
        finals,
        [VMEM] * 4,
        [VMEM],
        limit=8,
    )
    return (encoded[None], grad_w_o)


def attend_call(me_s, packets, weights, rows, width):
    group = 4 * HEAD_DIM
    shape = jax.ShapeDtypeStruct
    scratch = [VMEM((4, *packets[0].shape), BF16)]
    scratch += [VMEM(w.shape, w.dtype) for w in weights]
    scratch += [VMEM((4 * rows, width), BF16)]
    scratch += [VMEM((4, 4 * rows, group), BF16)] * 3
    scratch += [pltpu.SemaphoreType.DMA((10,))]
    arrays = [*packets, *weights]
    return local_call(
        functools.partial(attend_kernel, rows),
        [
            shape((4 * rows, group), BF16),
            *[shape((rows, group), BF16)] * 3,
            shape((rows, width), BF16),
        ],
        [me_s],
        arrays,
        [HBM] * len(arrays),
        [VMEM] * 5,
        scratch=scratch,
        limit=63,
        cost=100000000,
    )


def solution(mesh):
    in_specs = (
        P("clip", "tm", None),
        P("clip", "tm"),
        P("clip", "tm"),
        P(),
        P(),
        P(),
        P(None, "tm"),
        P("tm", None),
        P("clip", "tm", None),
    )
    out_specs = (P("clip", "tm", None), P("tm", None))
    on_line = mesh.shape["tm"] == 4 and mesh.shape["clip"] == 8
    return jax.shard_map(
        line_device if on_line else general_device,
        mesh=mesh,
        in_specs=in_specs,
        out_specs=out_specs,
        check_vma=False,
    )
```
